512 devices in a mesh: ctx: 64 (over y, z), tp: 8 (over x, core).
Axes of the slice: x: 4, y: 8, z: 8, core: 2. Of those that a mesh axis runs over, the one named last changes fastest.
Arguments:
- queries: bfloat16 [32768, 4096], P('ctx', 'tp'), may hold values from -400 to 400
- keys: bfloat16 [32768, 1024], P('ctx', 'tp'), may hold values from -6 to 6
- values: bfloat16 [32768, 1024], P('ctx', 'tp'), may hold values from -10 to 10
- gates: float32 [32], P('tp'), may hold values from -1 to 4
- out_weight: bfloat16 [4096, 4096], P('tp'), may hold values from -0.09375 to 0.09375
Outputs:
- mixed: bfloat16 [32768, 4096], P(('ctx', 'tp'))
The draws below stay inside these ranges and needn't reach their ends.
All inputs are finite; a program needn't handle non-finite values.
Results may differ from the reference program's by a relative error of at most 0.017.
Values may be sent and summed in bfloat16 or wider, within the bound.
No kernel may reach another device: no remote copies, remote signals or barrier semaphores. Data moves between devices by JAX's collectives and lax.ppermute only.
A program may use at most 128 MiB of HBM per device.

```python
import math
import jax
import jax.numpy as jnp
from jax import lax

D = 4096
H = 32
KVH = 8
HD = 128
SEGLEN = 2048
TOKENS = 32768
N_TP = 8


def class_ids(key):
    return jax.random.randint(jax.random.fold_in(key, 11), (TOKENS,), 0, 2 * HD)


def class_pattern(key):
    return jax.random.normal(jax.random.fold_in(key, 12), (2 * HD, KVH * HD), jnp.float32)


def offset_rows(key):
    offsets = jax.random.uniform(jax.random.fold_in(key, 14), (TOKENS // SEGLEN, KVH), jnp.float32, -3.0, -1.5)
    return jnp.repeat(offsets, SEGLEN, axis=0)


def shared_keys(key):
    pattern = jnp.take(class_pattern(key), class_ids(key), axis=0)
    noise_part = 0.5 * jax.random.normal(jax.random.fold_in(key, 13), (TOKENS, KVH * HD), jnp.float32)
    shifted = jnp.repeat(offset_rows(key), HD, axis=1)
    return 2.0 * pattern + noise_part + shifted


def probe_rows():
    return jnp.arange(TOKENS) % 4 == 2


def draw_keys(key, part):
    base_keys = shared_keys(key)
    return jnp.clip(base_keys, -6.0, 6.0).astype(jnp.bfloat16)


def draw_queries(key, part):
    own_key = jax.random.fold_in(key, 2)
    drawn_draw = jax.random.normal(own_key, (TOKENS, H * HD), jnp.float32)
    hot_dim = jax.random.randint(jax.random.fold_in(own_key, 4), (TOKENS, H, 1), 0, HD)
    hot_level = jax.random.uniform(jax.random.fold_in(own_key, 5), (TOKENS, H, 1), jnp.float32, 6.0, 10.0)
    cold_level = -jax.random.uniform(jax.random.fold_in(own_key, 6), (TOKENS, H, HD), jnp.float32, 4.0, 8.0)
    probe = jnp.where(jnp.arange(HD)[None, None, :] == hot_dim, hot_level, cold_level).reshape(TOKENS, H * HD)
    drawn_draw = jnp.where(probe_rows()[:, None], probe, drawn_draw)
    return jnp.clip(drawn_draw, -400.0, 400.0).astype(jnp.bfloat16)


def draw_values(key, part):
    token_class = class_ids(key)
    pattern = class_pattern(key)
    own_key = jax.random.fold_in(key, 3)
    segment_count = TOKENS // SEGLEN
    segment_of = jnp.arange(TOKENS) // SEGLEN
    segment_map = jax.random.normal(jax.random.fold_in(own_key, 9), (segment_count, 2 * HD, KVH * HD), jnp.float32)
    class_part = jnp.take(pattern, token_class, axis=0) + segment_map[segment_of, token_class]
    rising = 0.5 * (1.0 + 2.0 * jnp.arange(segment_count, dtype=jnp.float32) / (segment_count - 1))
    segment_means = jax.random.normal(jax.random.fold_in(own_key, 10), (segment_count, KVH * HD), jnp.float32) * rising[:, None]
    noise_key = jax.random.fold_in(own_key, 8)
    noise_part = jax.random.normal(noise_key, (TOKENS, KVH * HD), jnp.float32)
    combined = jnp.repeat(segment_means, SEGLEN, axis=0) + class_part + noise_part
    return jnp.clip(combined, -10.0, 10.0).astype(jnp.bfloat16)


def level_of(key, shape, split, low, largest):
    factor_of = 1.0
    for position, shards_of in split:
        draws = jax.random.uniform(jax.random.fold_in(jax.random.fold_in(key, 6), position), (shards_of,), jnp.float32, low / len(split), largest / len(split))
        factor_of = factor_of * jnp.repeat(jnp.exp(draws), shape[position] // shards_of).reshape((-1,) + (1,) * (len(shape) - 1 - position))
    return factor_of


def bell_draw(rng, shape, spread, reach, pieces=(), kind=jnp.bfloat16):
    result = spread * jax.random.normal(rng, shape, jnp.float32)
    if pieces:
        result = result * level_of(rng, shape, pieces, -0.22, 0.18)
    return jnp.clip(result, -reach, reach).astype(kind)


def setup_inputs(seed: int = 0) -> dict:
    arg_keys = jax.random.split(jax.random.key(seed), 6)
    return {
        "queries": draw_queries(jax.random.fold_in(arg_keys[5], 71), 0),
        "keys": draw_keys(jax.random.fold_in(arg_keys[5], 71), 0),
        "values": draw_values(jax.random.fold_in(arg_keys[5], 71), 0),
        "gates": jnp.clip(-1.0 + 5.0 * jax.random.uniform(arg_keys[3], (H,), jnp.float32) ** level_of(arg_keys[3], (H,), ((0, 8),), -0.2, 0.2), -1.0, 4.0),
        "out_weight": bell_draw(arg_keys[4], (H * HD, D), (H * HD) ** -0.5, 0.09375, ((0, 8),)),
    }


def feature_map(values_in):
    return jax.nn.elu(values_in.astype(jnp.float32)) + 1.0

def reference(queries, keys, values, gates, out_weight):
    group_size = H // KVH
    segment_count = TOKENS // SEGLEN
    query_seg = queries.reshape(segment_count, SEGLEN, KVH, group_size, HD)
    key_seg = keys.reshape(segment_count, SEGLEN, KVH, HD)
    value_seg = values.reshape(segment_count, SEGLEN, KVH, HD)
    key_feat = feature_map(key_seg)
    deltas = jnp.einsum('sjkd,sjke->skde', key_feat, value_seg.astype(jnp.float32), precision=lax.Precision.HIGHEST)
    norm_terms = lax.optimization_barrier(jnp.sum(key_feat, axis=1))
    memory_all = jnp.concatenate([jnp.zeros_like(deltas[:1]), jnp.cumsum(deltas, axis=0)[:-1]], axis=0)
    norm_all = jnp.concatenate([jnp.zeros_like(norm_terms[:1]), jnp.cumsum(norm_terms, axis=0)[:-1]], axis=0)
    gate_share = jax.nn.sigmoid(gates.astype(jnp.float32)).reshape(KVH, group_size)[None, :, :, None]
    causal = jnp.tril(jnp.ones((SEGLEN, SEGLEN), dtype=bool))

    def one_head_group(head_parts):
        query_part, key_part, value_part = head_parts
        scores = jnp.einsum('tgd,sd->gts', query_part.astype(jnp.float32), key_part.astype(jnp.float32)) / math.sqrt(HD)
        scores = jnp.where(causal[None], scores, -jnp.inf)
        row_max = lax.optimization_barrier(jnp.max(scores, axis=-1, keepdims=True))
        exponent = jnp.exp(scores - row_max)
        weights = (exponent / lax.optimization_barrier(jnp.sum(exponent, axis=-1, keepdims=True))).astype(jnp.bfloat16)
        return jnp.einsum('gts,se->tge', weights.astype(jnp.float32), value_part.astype(jnp.float32))

    def one_segment(segment_items):
        query_block, key_block, value_block, memory, norm_sum = segment_items
        query_feat = feature_map(query_block)
        numerator = jnp.einsum('tkgd,kde->tkge', query_feat, memory, precision=lax.Precision.HIGHEST)
        denominator = jnp.einsum('tkgd,kd->tkg', query_feat, norm_sum, precision=lax.Precision.HIGHEST)
        retrieved = numerator / jnp.maximum(denominator, 1.0)[..., None]
        local_out = lax.map(one_head_group, (query_block.transpose(1, 0, 2, 3), key_block.transpose(1, 0, 2), value_block.transpose(1, 0, 2)))
        local_out = local_out.transpose(1, 0, 2, 3)
        mixed_heads = gate_share * retrieved + (1.0 - gate_share) * local_out
        return mixed_heads.astype(jnp.bfloat16).reshape(SEGLEN, H * HD)
    attended = lax.map(one_segment, (query_seg, key_seg, value_seg, memory_all, norm_all)).reshape(TOKENS, H * HD)
    width_dev = H * HD // N_TP
    running = jnp.zeros((TOKENS, D), jnp.float32)
    for part_index in range(N_TP):
        partial_term = jnp.dot(attended[:, part_index * width_dev:(part_index + 1) * width_dev], out_weight[part_index * width_dev:(part_index + 1) * width_dev], preferred_element_type=jnp.float32)
        rounded = lax.optimization_barrier(partial_term.astype(jnp.bfloat16))
        running = running + rounded.astype(jnp.float32)
    return running.astype(jnp.bfloat16)
```

```python
import functools
import math

import jax
import jax.numpy as jnp
from jax import lax
from jax.experimental import pallas as pl
from jax.experimental.pallas import tpu as pltpu
from jax.sharding import PartitionSpec as P

H = 32
KVH = 8
HD = 128
GROUP = H // KVH
ROWS = 512
SPAN = 4
BLOCK = 64
N_CTX = 64
N_TP = 8
CHUNK = 256
LOG2E = 1.4426950408889634
SCALE = LOG2E / math.sqrt(HD)
MASKED = -1e30
F32 = jnp.float32
BF16 = jnp.bfloat16
VM = pl.BlockSpec(memory_space=pltpu.VMEM)
SM = pl.BlockSpec(memory_space=pltpu.SMEM)
NT = (((1,), (1,)), ((), ()))
TN = (((0,), (0,)), ((), ()))


def feature_map(x):
    return jnp.where(x > 0.0, x + 1.0, jnp.exp(jnp.minimum(x, 0.0)))


def split_two(x):
    high = x.astype(BF16)
    return high, (x - high.astype(F32)).astype(BF16)


def call(kernel, out_shape, cost, **kw):
    flops, read, exps = cost
    return pl.pallas_call(
        kernel,
        out_shape=out_shape,
        compiler_params=pltpu.CompilerParams(vmem_limit_bytes=24 * 1024 * 1024),
        cost_estimate=pl.CostEstimate(flops=flops, bytes_accessed=read, transcendentals=exps),
        **kw,
    )


def delta_kernel(k_ref, v_ref, kv_ref, d_ref):
    k = k_ref[...]
    v = v_ref[...]
    kv_ref[:, :HD] = k
    kv_ref[:, HD:] = v
    feat = feature_map(k.astype(F32))
    high, low = split_two(feat)
    d_ref[:HD, :] = lax.dot_general(v, high, TN, preferred_element_type=F32) + lax.dot_general(
        v, low, TN, preferred_element_type=F32
    )
    d_ref[HD:, :] = jnp.broadcast_to(jnp.sum(feat, axis=0, keepdims=True), (8, HD))


def delta_call(keys, values):
    return call(
        delta_kernel,
        (jax.ShapeDtypeStruct((ROWS, 2 * HD), BF16), jax.ShapeDtypeStruct((HD + 8, HD), F32)),
        (2 * 2 * ROWS * HD * HD, 600000, ROWS * HD),
        in_specs=[VM, VM],
        out_specs=(VM, VM),
    )(keys, values)


def values_and_ones(v):
    return jnp.concatenate([v, jnp.ones_like(v)], axis=1)


def own_kernel(q_ref, k_ref, v_ref, acc_ref, top_ref):
    k = k_ref[...]
    wide = values_and_ones(v_ref[...])
    for r in range(ROWS // CHUNK):
        rows = slice(r * CHUNK, (r + 1) * CHUNK)
        seen = (r + 1) * CHUNK
        query_pos = r * CHUNK + lax.broadcasted_iota(jnp.int32, (CHUNK, seen), 0)
        key_pos = lax.broadcasted_iota(jnp.int32, (CHUNK, seen), 1)
        visible = key_pos <= query_pos
        for h in range(GROUP):
            q = q_ref[rows, h * HD : (h + 1) * HD]
            s = lax.dot_general(q, k[:seen], NT, preferred_element_type=F32)
            s = jnp.where(visible, s, MASKED)
            top = jnp.max(s, axis=1, keepdims=True)
            p = jnp.exp2((s - top) * SCALE).astype(BF16)
            acc_ref[h, rows, :] = jnp.dot(p, wide[:seen], preferred_element_type=F32)
            top_ref[h, rows, :] = jnp.broadcast_to(top, (CHUNK, HD))


def own_call(queries, keys, values):
    return call(
        own_kernel,
        (
            jax.ShapeDtypeStruct((GROUP, ROWS, 2 * HD), F32),
            jax.ShapeDtypeStruct((GROUP, ROWS, HD), F32),
        ),
        (GROUP * ROWS * ROWS * HD * 4, 4000000, GROUP * ROWS * ROWS),
        in_specs=[VM, VM, VM],
        out_specs=(VM, VM),
    )(queries, keys, values)


def last_kernel(
    place_ref, gate_ref, q_ref, kv1_ref, kv2_ref, kv3_ref, acc_in, top_in, mem_ref, keep_ref, send_ref, acc_ref, top_ref, out_ref
):
    position = place_ref[0]
    x = place_ref[1]
    core = place_ref[2]
    acc_ref[...] = acc_in[...]
    top_ref[...] = top_in[...]
    for d, kv_ref in ((1, kv1_ref), (2, kv2_ref), (3, kv3_ref)):

        @pl.when(position >= d)
        def _():
            k = kv_ref[:, :HD]
            wide = values_and_ones(kv_ref[:, HD:])
            for r in range(ROWS // CHUNK):
                rows = slice(r * CHUNK, (r + 1) * CHUNK)
                for h in range(GROUP):
                    q = q_ref[rows, h * HD : (h + 1) * HD]
                    s = lax.dot_general(q, k, NT, preferred_element_type=F32)
                    before = top_ref[h, rows, :]
                    top = jnp.maximum(before, jnp.max(s, axis=1, keepdims=True))
                    shrink = jnp.exp2((before - top) * SCALE)
                    p = jnp.exp2((s - top[:, :1]) * SCALE).astype(BF16)
                    pv = jnp.dot(p, wide, preferred_element_type=F32)
                    acc_ref[h, rows, :] = acc_ref[h, rows, :] * jnp.concatenate([shrink, shrink], axis=1) + pv
                    top_ref[h, rows, :] = top

    mem = jnp.concatenate(
        [mem_ref[:HD, :], jnp.broadcast_to(mem_ref[HD : HD + 1, :], (HD, HD))], axis=0
    )
    mem_high, mem_low = split_two(mem)
    mem_twice = jnp.concatenate([mem_high, mem_high], axis=1)
    for h in range(GROUP):
        gate = jax.nn.sigmoid(jnp.full((1, HD), gate_ref[h], F32))
        feat = feature_map(q_ref[:, h * HD : (h + 1) * HD].astype(F32))
        high, low = split_two(feat)
        both = jnp.concatenate([high, low], axis=1)
        read = lax.dot_general(both, mem_twice, NT, preferred_element_type=F32)
        read = read + lax.dot_general(high, mem_low, NT, preferred_element_type=F32)
        retrieved = read[:, :HD] / jnp.maximum(read[:, HD:], 1.0)
        local = acc_ref[h, :, :HD] / acc_ref[h, :, HD:]
        out_ref[:, h * HD : (h + 1) * HD] = (gate * retrieved + (1.0 - gate) * local).astype(BF16)
    for b in range(N_TP // 2):
        mine = pl.multiple_of((2 * b + core) * BLOCK, BLOCK)
        other = pl.multiple_of((2 * b + 1 - core) * BLOCK, BLOCK)
        keep_ref[b * BLOCK : (b + 1) * BLOCK, :] = out_ref[pl.ds(mine, BLOCK), :]
        send_ref[b * BLOCK : (b + 1) * BLOCK, :] = out_ref[pl.ds(other, BLOCK), :]


def last_call(place, gates, queries, kv1, kv2, kv3, acc, top, mem):
    half = jax.ShapeDtypeStruct((ROWS // 2, GROUP * HD), BF16)
    return call(
        last_kernel,
        (half, half),
        (3 * GROUP * ROWS * ROWS * HD * 4, 6000000, 3 * GROUP * ROWS * ROWS),
        in_specs=[SM, SM] + [VM] * 7,
        out_specs=(VM, VM),
        scratch_shapes=[
            pltpu.VMEM((GROUP, ROWS, 2 * HD), F32),
            pltpu.VMEM((GROUP, ROWS, HD), F32),
            pltpu.VMEM((ROWS, GROUP * HD), BF16),
        ],
    )(place, gates, queries, kv1, kv2, kv3, acc, top, mem)


def project_kernel(keep_ref, got_ref, w_own_ref, w_other_ref, out_ref):
    out = jnp.dot(keep_ref[...], w_own_ref[...], preferred_element_type=F32)
    out = out + jnp.dot(got_ref[...], w_other_ref[...], preferred_element_type=F32)
    out_ref[...] = out.astype(BF16)


def project_call(keep, got, w_own, w_other):
    rows, depth = keep.shape
    width = w_own.shape[1]
    tile = 512
    whole = pl.BlockSpec((rows, depth), lambda j: (0, 0))
    strip = pl.BlockSpec((depth, tile), lambda j: (0, j))
    return call(
        project_kernel,
        jax.ShapeDtypeStruct((rows, width), BF16),
        (4 * rows * depth * width, 12000000, 0),
        grid=(width // tile,),
        in_specs=[whole, whole, strip, strip],
        out_specs=pl.BlockSpec((rows, tile), lambda j: (0, j)),
    )(keep, got, w_own, w_other)


def along_z(step):
    return [(i, i + step) for i in range(N_CTX) if i // SPAN == (i + step) // SPAN]


def along_y(step):
    return [(i, i + 8 * step) for i in range(N_CTX - 8 * step)]


def swap(bit, size):
    return [(i, i ^ bit) for i in range(size)]


def on_device(queries, keys, values, gates, out_weight):
    ctx = lax.axis_index("ctx")
    tp = lax.axis_index("tp")
    place = jnp.stack([ctx % SPAN, tp // 2, tp % 2]).astype(jnp.int32)
    kv, delta = delta_call(keys, values)
    kv1, kv2, kv3 = [lax.ppermute(kv, "ctx", along_z(d)) for d in (1, 2, 3)]
    w_other = lax.ppermute(out_weight, "tp", swap(1, N_TP))
    before = lax.ppermute(delta, "ctx", along_y(1))
    before = before + lax.ppermute(delta + before, "ctx", along_y(2))
    before = before + lax.ppermute(delta + before, "ctx", along_y(4))
    lower = (ctx % 8) < SPAN
    mem = before + lax.ppermute(before + jnp.where(lower, delta, 0.0), "ctx", swap(4, N_CTX))
    mem = mem + lax.ppermute(mem, "ctx", swap(1, N_CTX))
    mem = mem + lax.ppermute(mem, "ctx", swap(2, N_CTX))
    acc, top = own_call(queries, keys, values)
    keep, send = last_call(place, gates, queries, kv1, kv2, kv3, acc, top, mem)
    got = lax.ppermute(send, "tp", swap(1, N_TP))
    partial = project_call(keep, got, out_weight, w_other)
    parts = lax.all_to_all(
        partial.reshape(N_TP // 2, BLOCK, -1), "tp", 0, 0, tiled=True,
        axis_index_groups=[[0, 2, 4, 6], [1, 3, 5, 7]],
    )
    return jnp.sum(parts.astype(F32), axis=0).astype(BF16)


def solution(mesh):
    placed = (P("ctx", "tp"), P("ctx", "tp"), P("ctx", "tp"), P("tp"), P("tp", None))
    return jax.shard_map(
        on_device, mesh=mesh, in_specs=placed, out_specs=P(("ctx", "tp"), None), check_vma=False
    )
```

```python
import functools
import math

import jax
import jax.numpy as jnp
from jax import lax
from jax.experimental import pallas as pl
from jax.experimental.pallas import tpu as pltpu
from jax.sharding import PartitionSpec as P

H = 32
KVH = 8
HD = 128
GROUP = H // KVH
ROWS = 512
SPAN = 4
BLOCK = 64
N_CTX = 64
N_TP = 8
CHUNK = 256
LOG2E = 1.4426950408889634
SCALE = LOG2E / math.sqrt(HD)
MASKED = -1e30
F32 = jnp.float32
BF16 = jnp.bfloat16
VM = pl.BlockSpec(memory_space=pltpu.VMEM)
SM = pl.BlockSpec(memory_space=pltpu.SMEM)
NT = (((1,), (1,)), ((), ()))
TN = (((0,), (0,)), ((), ()))


def feature_map(x):
    return jnp.where(x > 0.0, x + 1.0, jnp.exp(jnp.minimum(x, 0.0)))


def split_two(x):
    high = x.astype(BF16)
    return high, (x - high.astype(F32)).astype(BF16)


def call(kernel, out_shape, cost, **kw):
    flops, read, exps = cost
    return pl.pallas_call(
        kernel,
        out_shape=out_shape,
        compiler_params=pltpu.CompilerParams(vmem_limit_bytes=24 * 1024 * 1024),
        cost_estimate=pl.CostEstimate(flops=flops, bytes_accessed=read, transcendentals=exps),
        **kw,
    )


def delta_kernel(k_ref, v_ref, kv_ref, d_ref):
    k = k_ref[...]
    v = v_ref[...]
    kv_ref[:, :HD] = k
    kv_ref[:, HD:] = v
    feat = feature_map(k.astype(F32))
    high, low = split_two(feat)
    d_ref[:HD, :] = lax.dot_general(v, high, TN, preferred_element_type=F32) + lax.dot_general(
        v, low, TN, preferred_element_type=F32
    )
    d_ref[HD:, :] = jnp.broadcast_to(jnp.sum(feat, axis=0, keepdims=True), (16, HD))


def delta_call(keys, values):
    return call(
        delta_kernel,
        (jax.ShapeDtypeStruct((ROWS, 2 * HD), BF16), jax.ShapeDtypeStruct((HD + 16, HD), F32)),
        (2 * 2 * ROWS * HD * HD, 600000, ROWS * HD),
        in_specs=[VM, VM],
        out_specs=(VM, VM),
    )(keys, values)


def values_and_ones(v):
    return jnp.concatenate([v, jnp.ones_like(v)], axis=1)


def own_kernel(q_ref, k_ref, v_ref, acc_ref, top_ref):
    k = k_ref[...]
    wide = values_and_ones(v_ref[...])
    for r in range(ROWS // CHUNK):
        rows = slice(r * CHUNK, (r + 1) * CHUNK)
        seen = (r + 1) * CHUNK
        query_pos = r * CHUNK + lax.broadcasted_iota(jnp.int32, (CHUNK, seen), 0)
        key_pos = lax.broadcasted_iota(jnp.int32, (CHUNK, seen), 1)
        visible = key_pos <= query_pos
        for h in range(GROUP):
            q = q_ref[rows, h * HD : (h + 1) * HD]
            s = lax.dot_general(q, k[:seen], NT, preferred_element_type=F32)
            s = jnp.where(visible, s, MASKED)
            top = jnp.max(s, axis=1, keepdims=True)
            p = jnp.exp2((s - top) * SCALE).astype(BF16)
            acc_ref[h, rows, :] = jnp.dot(p, wide[:seen], preferred_element_type=F32)
            top_ref[h, rows, :] = jnp.broadcast_to(top, (CHUNK, HD))


def own_call(queries, keys, values):
    return call(
        own_kernel,
        (
            jax.ShapeDtypeStruct((GROUP, ROWS, 2 * HD), F32),
            jax.ShapeDtypeStruct((GROUP, ROWS, HD), F32),
        ),
        (GROUP * ROWS * ROWS * HD * 4, 4000000, GROUP * ROWS * ROWS),
        in_specs=[VM, VM, VM],
        out_specs=(VM, VM),
    )(queries, keys, values)


def step_kernel(distance, place_ref, q_ref, kv_ref, acc_in, top_in, acc_ref, top_ref):
    @pl.when(place_ref[0] >= distance)
    def _():
        k = kv_ref[:, :HD]
        wide = values_and_ones(kv_ref[:, HD:])
        for r in range(ROWS // CHUNK):
            rows = slice(r * CHUNK, (r + 1) * CHUNK)
            for h in range(GROUP):
                q = q_ref[rows, h * HD : (h + 1) * HD]
                s = lax.dot_general(q, k, NT, preferred_element_type=F32)
                before = top_in[h, rows, :]
                top = jnp.maximum(before, jnp.max(s, axis=1, keepdims=True))
                shrink = jnp.exp2((before - top) * SCALE)
                p = jnp.exp2((s - top[:, :1]) * SCALE).astype(BF16)
                pv = jnp.dot(p, wide, preferred_element_type=F32)
                acc_ref[h, rows, :] = acc_in[h, rows, :] * jnp.concatenate([shrink, shrink], axis=1) + pv
                top_ref[h, rows, :] = top


def step_call(distance, place, queries, kv, acc, top):
    return call(
        functools.partial(step_kernel, distance),
        (
            jax.ShapeDtypeStruct((GROUP, ROWS, 2 * HD), F32),
            jax.ShapeDtypeStruct((GROUP, ROWS, HD), F32),
        ),
        (GROUP * ROWS * ROWS * HD * 4, 4000000, GROUP * ROWS * ROWS),
        in_specs=[SM] + [VM] * 4,
        out_specs=(VM, VM),
        input_output_aliases={3: 0, 4: 1},
    )(place, queries, kv, acc, top)


def merge_kernel(place_ref, gate_ref, q_ref, acc_ref, mem_a, mem_b, keep_ref, send_ref, out_ref):
    x = place_ref[1]
    core = place_ref[2]
    mem = mem_a[...] + mem_b[...].astype(F32)
    mem = jnp.concatenate([mem[:HD, :], jnp.broadcast_to(mem[HD : HD + 1, :], (HD, HD))], axis=0)
    mem_high, mem_low = split_two(mem)
    mem_twice = jnp.concatenate([mem_high, mem_high], axis=1)
    for h in range(GROUP):
        gate = jax.nn.sigmoid(jnp.full((1, HD), gate_ref[h], F32))
        feat = feature_map(q_ref[:, h * HD : (h + 1) * HD].astype(F32))
        high, low = split_two(feat)
        both = jnp.concatenate([high, low], axis=1)
        read = lax.dot_general(both, mem_twice, NT, preferred_element_type=F32)
        read = read + lax.dot_general(high, mem_low, NT, preferred_element_type=F32)
        retrieved = read[:, :HD] / jnp.maximum(read[:, HD:], 1.0)
        local = acc_ref[h, :, :HD] / acc_ref[h, :, HD:]
        out_ref[:, h * HD : (h + 1) * HD] = (gate * retrieved + (1.0 - gate) * local).astype(BF16)
    for b in range(N_TP // 2):
        chip = (x + b) % (N_TP // 2)
        mine = pl.multiple_of((2 * chip + core) * BLOCK, BLOCK)
        other = pl.multiple_of((2 * chip + 1 - core) * BLOCK, BLOCK)
        keep_ref[b * BLOCK : (b + 1) * BLOCK, :] = out_ref[pl.ds(mine, BLOCK), :]
        send_ref[b * BLOCK : (b + 1) * BLOCK, :] = out_ref[pl.ds(other, BLOCK), :]


def merge_call(place, gates, queries, acc, mem_a, mem_b):
    half = jax.ShapeDtypeStruct((ROWS // 2, GROUP * HD), BF16)
    return call(
        merge_kernel,
        (half, half),
        (6 * ROWS * GROUP * HD * HD * 2, 4000000, ROWS * GROUP * HD),
        in_specs=[SM, SM] + [VM] * 4,
        out_specs=(VM, VM),
        scratch_shapes=[pltpu.VMEM((ROWS, GROUP * HD), BF16)],
    )(place, gates, queries, acc, mem_a, mem_b)


def project_kernel(keep_ref, got_ref, w_own_ref, w_other_ref, own_ref, right_ref, left_ref, far_a_ref, far_b_ref):
    width = w_own_ref.shape[1]
    tile = 512
    for j in range(width // tile):
        cols = slice(j * tile, (j + 1) * tile)
        out = jnp.dot(keep_ref[...], w_own_ref[:, cols], preferred_element_type=F32)
        out = out + jnp.dot(got_ref[...], w_other_ref[:, cols], preferred_element_type=F32)
        out = out.astype(BF16)
        own_ref[:, cols] = out[:BLOCK]
        right_ref[:, cols] = out[BLOCK : 2 * BLOCK]
        left_ref[:, cols] = out[3 * BLOCK :]
        far_ref = far_a_ref if j < width // tile // 2 else far_b_ref
        at = j % (width // tile // 2) * tile
        far_ref[:, at : at + tile] = out[2 * BLOCK : 3 * BLOCK]


def project_call(keep, got, w_own, w_other):
    rows, depth = keep.shape
    width = w_own.shape[1]
    whole = jax.ShapeDtypeStruct((BLOCK, width), BF16)
    half = jax.ShapeDtypeStruct((BLOCK, width // 2), BF16)
    return call(
        project_kernel,
        (whole, whole, whole, half, half),
        (4 * rows * depth * width, 12000000, 0),
        in_specs=[VM] * 4,
        out_specs=(VM,) * 5,
    )(keep, got, w_own, w_other)


def along_z(step):
    return [(i, i + step) for i in range(N_CTX) if i // SPAN == (i + step) // SPAN]


def along_y(step):
    return [(i, i + 8 * step) for i in range(N_CTX - 8 * step)]


def swap(bit, size):
    return [(i, i ^ bit) for i in range(size)]


def after(x, *others):
    return lax.optimization_barrier((x, others))[0]


def turned(step):
    return [(i, (i + 2 * step) % N_TP) for i in range(N_TP)]


def on_device(queries, keys, values, gates, out_weight):
    ctx = lax.axis_index("ctx")
    tp = lax.axis_index("tp")
    place = jnp.stack([ctx % SPAN, tp // 2, tp % 2]).astype(jnp.int32)
    send = lambda x, route: lax.ppermute(x.astype(BF16), "ctx", route)
    kv, delta = delta_call(keys, values)
    kv1, kv2, kv3 = [send(kv, along_z(d)) for d in (1, 2, 3)]
    got = send(delta, along_y(1))
    acc, top = own_call(queries, keys, values)
    before = after(got, acc).astype(F32)
    got = send(delta + before, along_y(2))
    acc, top = step_call(1, place, queries, kv1, acc, top)
    before = before + after(got, acc).astype(F32)
    got = send(delta + before, along_y(4))
    acc, top = step_call(2, place, queries, kv2, acc, top)
    before = before + after(got, acc).astype(F32)
    lower = (ctx % 8) < SPAN
    got = send(before + jnp.where(lower, delta, 0.0), swap(4, N_CTX))
    acc, top = step_call(3, place, queries, kv3, acc, top)
    mem = before + after(got, acc).astype(F32)
    got = send(mem, swap(1, N_CTX))
    w_other = lax.ppermute(out_weight, "tp", swap(1, N_TP))
    mem = mem + after(got, w_other).astype(F32)
    got = send(mem, swap(2, N_CTX))
    keep, give = merge_call(place, gates, queries, acc, mem, got)
    got = lax.ppermute(give, "tp", swap(1, N_TP))
    own, right, left, far_a, far_b = project_call(keep, got, out_weight, w_other)
    from_left = lax.ppermute(far_a, "tp", turned(1))
    from_right = lax.ppermute(far_b, "tp", turned(-1))
    half = far_a.shape[1]
    right = jnp.concatenate([right[:, :half] + from_left, right[:, half:]], axis=1)
    left = jnp.concatenate([left[:, :half], left[:, half:] + from_right], axis=1)
    from_left = lax.ppermute(right, "tp", turned(1))
    from_right = lax.ppermute(left, "tp", turned(-1))
    return (own.astype(F32) + from_left.astype(F32) + from_right.astype(F32)).astype(BF16)


def solution(mesh):
    placed = (P("ctx", "tp"), P("ctx", "tp"), P("ctx", "tp"), P("tp"), P("tp", None))
    return jax.shard_map(
        on_device, mesh=mesh, in_specs=placed, out_specs=P(("ctx", "tp"), None), check_vma=False
    )
```

```python
import functools
import math

import jax
import jax.numpy as jnp
from jax import lax
from jax.experimental import pallas as pl
from jax.experimental.pallas import tpu as pltpu
from jax.sharding import PartitionSpec as P

H = 32
KVH = 8
HD = 128
GROUP = H // KVH
ROWS = 512
SPAN = 4
BLOCK = 64
N_CTX = 64
N_TP = 8
CHUNK = 256
LOG2E = 1.4426950408889634
SCALE = LOG2E / math.sqrt(HD)
MASKED = -1e30
F32 = jnp.float32
BF16 = jnp.bfloat16
VM = pl.BlockSpec(memory_space=pltpu.VMEM)
SM = pl.BlockSpec(memory_space=pltpu.SMEM)
NT = (((1,), (1,)), ((), ()))
TN = (((0,), (0,)), ((), ()))


def feature_map(x):
    return jnp.where(x > 0.0, x + 1.0, jnp.exp(jnp.minimum(x, 0.0)))


def split_two(x):
    high = x.astype(BF16)
    return high, (x - high.astype(F32)).astype(BF16)


def call(kernel, out_shape, cost, **kw):
    flops, read, exps = cost
    return pl.pallas_call(
        kernel,
        out_shape=out_shape,
        compiler_params=pltpu.CompilerParams(vmem_limit_bytes=24 * 1024 * 1024),
        cost_estimate=pl.CostEstimate(flops=flops, bytes_accessed=read, transcendentals=exps),
        **kw,
    )


def delta_kernel(kv_ref, d_ref, d16_ref):
    v = kv_ref[:, HD:]
    feat = feature_map(kv_ref[:, :HD].astype(F32))
    high, low = split_two(feat)
    delta = lax.dot_general(v, high, TN, preferred_element_type=F32) + lax.dot_general(
        v, low, TN, preferred_element_type=F32
    )
    norm = jnp.broadcast_to(jnp.sum(feat, axis=0, keepdims=True), (16, HD))
    d_ref[:HD, :] = delta
    d_ref[HD:, :] = norm
    d16_ref[:HD, :] = delta.astype(BF16)
    d16_ref[HD:, :] = norm.astype(BF16)


def delta_call(kv):
    return call(
        delta_kernel,
        (jax.ShapeDtypeStruct((HD + 16, HD), F32), jax.ShapeDtypeStruct((HD + 16, HD), BF16)),
        (2 * 2 * ROWS * HD * HD, 400000, ROWS * HD),
        in_specs=[VM],
        out_specs=(VM, VM),
    )(kv)


def values_and_ones(v):
    return jnp.concatenate([v, jnp.ones_like(v)], axis=1)


def own_kernel(q_ref, kv_ref, acc_ref, top_ref):
    k = kv_ref[:, :HD]
    wide = values_and_ones(kv_ref[:, HD:])
    for r in range(ROWS // CHUNK):
        rows = slice(r * CHUNK, (r + 1) * CHUNK)
        seen = (r + 1) * CHUNK
        query_pos = r * CHUNK + lax.broadcasted_iota(jnp.int32, (CHUNK, seen), 0)
        key_pos = lax.broadcasted_iota(jnp.int32, (CHUNK, seen), 1)
        visible = key_pos <= query_pos
        for h in range(GROUP):
            q = q_ref[rows, h * HD : (h + 1) * HD]
            s = lax.dot_general(q, k[:seen], NT, preferred_element_type=F32)
            s = jnp.where(visible, s, MASKED)
            top = jnp.max(s, axis=1, keepdims=True)
            p = jnp.exp2((s - top) * SCALE).astype(BF16)
            acc_ref[h, rows, :] = jnp.dot(p, wide[:seen], preferred_element_type=F32)
            top_ref[h, rows, :] = jnp.broadcast_to(top, (CHUNK, HD))


def own_call(queries, kv):
    return call(
        own_kernel,
        (
            jax.ShapeDtypeStruct((GROUP, ROWS, 2 * HD), F32),
            jax.ShapeDtypeStruct((GROUP, ROWS, HD), F32),
        ),
        (GROUP * ROWS * ROWS * HD * 4, 4000000, GROUP * ROWS * ROWS),
        in_specs=[VM, VM],
        out_specs=(VM, VM),
    )(queries, kv)


def step_kernel(distance, place_ref, q_ref, kv_ref, acc_in, top_in, acc_ref, top_ref):
    @pl.when(place_ref[0] >= distance)
    def _():
        k = kv_ref[:, :HD]
        wide = values_and_ones(kv_ref[:, HD:])
        for r in range(ROWS // CHUNK):
            rows = slice(r * CHUNK, (r + 1) * CHUNK)
            for h in range(GROUP):
                q = q_ref[rows, h * HD : (h + 1) * HD]
                s = lax.dot_general(q, k, NT, preferred_element_type=F32)
                before = top_in[h, rows, :]
                top = jnp.maximum(before, jnp.max(s, axis=1, keepdims=True))
                shrink = jnp.exp2((before - top) * SCALE)
                p = jnp.exp2((s - jnp.concatenate([top] * SPAN, axis=1)) * SCALE).astype(BF16)
                pv = jnp.dot(p, wide, preferred_element_type=F32)
                acc_ref[h, rows, :] = acc_in[h, rows, :] * jnp.concatenate([shrink, shrink], axis=1) + pv
                top_ref[h, rows, :] = top

    @pl.when(place_ref[0] < distance)
    def _():
        acc_ref[...] = acc_in[...]
        top_ref[...] = top_in[...]


def step_call(distance, place, queries, kv, acc, top):
    return call(
        functools.partial(step_kernel, distance),
        (
            jax.ShapeDtypeStruct((GROUP, ROWS, 2 * HD), F32),
            jax.ShapeDtypeStruct((GROUP, ROWS, HD), F32),
        ),
        (GROUP * ROWS * ROWS * HD * 4, 4000000, GROUP * ROWS * ROWS),
        in_specs=[SM] + [VM] * 4,
        out_specs=(VM, VM),
    )(place, queries, kv, acc, top)


def merge_kernel(place_ref, gate_ref, q_ref, acc_ref, mem0, mem1, mem2, mem3, keep_ref, send_ref, out_ref):
    x = place_ref[1]
    core = place_ref[2]
    mem = mem0[...] + mem1[...].astype(F32) + (mem2[...].astype(F32) + mem3[...].astype(F32))
    mem = jnp.concatenate([mem[:HD, :], jnp.broadcast_to(mem[HD : HD + 1, :], (HD, HD))], axis=0)
    mem_high, mem_low = split_two(mem)
    mem_twice = jnp.concatenate([mem_high, mem_high], axis=1)
    for h in range(GROUP):
        gate = jax.nn.sigmoid(jnp.full((1, HD), gate_ref[h], F32))
        feat = feature_map(q_ref[:, h * HD : (h + 1) * HD].astype(F32))
        high, low = split_two(feat)
        both = jnp.concatenate([high, low], axis=1)
        read = lax.dot_general(both, mem_twice, NT, preferred_element_type=F32)
        read = read + lax.dot_general(high, mem_low, NT, preferred_element_type=F32)
        retrieved = read[:, :HD] / jnp.maximum(read[:, HD:], 1.0)
        local = acc_ref[h, :, :HD] / acc_ref[h, :, HD:]
        out_ref[:, h * HD : (h + 1) * HD] = (gate * retrieved + (1.0 - gate) * local).astype(BF16)
    for b in range(N_TP // 2):
        chip = (x + b) % (N_TP // 2)
        mine = pl.multiple_of((2 * chip + core) * BLOCK, BLOCK)
        other = pl.multiple_of((2 * chip + 1 - core) * BLOCK, BLOCK)
        keep_ref[b * BLOCK : (b + 1) * BLOCK, :] = out_ref[pl.ds(mine, BLOCK), :]
        send_ref[b * BLOCK : (b + 1) * BLOCK, :] = out_ref[pl.ds(other, BLOCK), :]


def merge_call(place, gates, queries, acc, mems):
    half = jax.ShapeDtypeStruct((ROWS // 2, GROUP * HD), BF16)
    return call(
        merge_kernel,
        (half, half),
        (6 * ROWS * GROUP * HD * HD * 2, 4000000, ROWS * GROUP * HD),
        in_specs=[SM, SM] + [VM] * 6,
        out_specs=(VM, VM),
        scratch_shapes=[pltpu.VMEM((ROWS, GROUP * HD), BF16)],
    )(place, gates, queries, acc, *mems)


def project_kernel(first, keep_ref, got_ref, w_own_ref, w_other_ref, own_ref, right_ref, far_ref, left_ref):
    width = own_ref.shape[1]
    tile = 512
    for j in range(width // tile):
        cols = slice(j * tile, (j + 1) * tile)
        from_w = slice(first + j * tile, first + (j + 1) * tile)
        out = jnp.dot(keep_ref[...], w_own_ref[:, from_w], preferred_element_type=F32)
        out = out + jnp.dot(got_ref[...], w_other_ref[:, from_w], preferred_element_type=F32)
        out = out.astype(BF16)
        for b, ref in enumerate((own_ref, right_ref, far_ref, left_ref)):
            ref[:, cols] = out[b * BLOCK : (b + 1) * BLOCK]


def project_call(first, keep, got, w_own, w_other):
    rows, depth = keep.shape
    half = w_own.shape[1] // 2
    return call(
        functools.partial(project_kernel, first),
        (jax.ShapeDtypeStruct((BLOCK, half), BF16),) * 4,
        (4 * rows * depth * half, 6000000, 0),
        in_specs=[VM] * 4,
        out_specs=(VM,) * 4,
    )(keep, got, w_own, w_other)


def total_kernel(own_a, left_a, right_a, own_b, left_b, right_b, out_ref):
    half = own_a.shape[1]
    for first, parts in ((0, (own_a, left_a, right_a)), (half, (own_b, left_b, right_b))):
        total = parts[0][...].astype(F32) + parts[1][...].astype(F32) + parts[2][...].astype(F32)
        out_ref[:, first : first + half] = total.astype(BF16)


def total_call(*parts):
    rows, half = parts[0].shape
    return call(
        total_kernel,
        jax.ShapeDtypeStruct((rows, 2 * half), BF16),
        (6 * rows * half, 2000000, 0),
        in_specs=[VM] * 6,
        out_specs=VM,
    )(*parts)


def along_z(step):
    return [(i, i + step) for i in range(N_CTX) if i // SPAN == (i + step) // SPAN]


def along_y(step):
    return [(i, i + 8 * step) for i in range(N_CTX - 8 * step)]


def swap(bit, size):
    return [(i, i ^ bit) for i in range(size)]


def after(x, *others):
    return lax.optimization_barrier((x, others))[0]


def turned(step):
    return [(i, (i + 2 * step) % N_TP) for i in range(N_TP)]


def on_device(queries, keys, values, gates, out_weight):
    ctx = lax.axis_index("ctx")
    tp = lax.axis_index("tp")
    place = jnp.stack([ctx % SPAN, tp // 2, tp % 2]).astype(jnp.int32)
    send = lambda x, route: lax.ppermute(x.astype(BF16), "ctx", route)
    kv = jnp.concatenate([keys, values], axis=1)
    delta, delta16 = delta_call(kv)
    kv1 = send(kv, along_z(1))
    got = send(delta16, along_y(1))
    before = got.astype(F32)
    kv2 = send(after(kv, got), along_z(2))
    got = send(delta + before, along_y(2))
    acc, top = own_call(queries, kv)
    kv3 = send(after(kv, got), along_z(3))
    w_other = lax.ppermute(out_weight, "tp", swap(1, N_TP))
    before = before + after(got, acc).astype(F32)
    got = send(delta + before, along_y(4))
    acc, top = step_call(1, place, queries, kv1, acc, top)
    before = before + after(got, acc).astype(F32)
    lower = (ctx % 8) < SPAN
    got = send(before + jnp.where(lower, delta, 0.0), swap(4, N_CTX))
    acc, top = step_call(2, place, queries, kv2, acc, top)
    mem = before + after(got, acc).astype(F32)
    mem16 = mem.astype(BF16)
    mems = [send(mem16, swap(k, N_CTX)) for k in (1, 2, 3)]
    acc, top = step_call(3, place, queries, kv3, acc, top)
    mems = [after(m, acc) for m in mems]
    keep, give = merge_call(place, gates, queries, acc, [mem] + mems)
    got = lax.ppermute(give, "tp", swap(1, N_TP))
    own_a, right_a, far_a, left_a = project_call(0, keep, got, out_weight, w_other)
    far_a = lax.ppermute(far_a, "tp", turned(1))
    left_a = lax.ppermute(left_a, "tp", turned(-1))
    own_b, right_b, far_b, left_b = project_call(own_a.shape[1], keep, got, out_weight, w_other)
    far_b = lax.ppermute(far_b, "tp", turned(-1))
    right_b = lax.ppermute(right_b, "tp", turned(1))
    right_a = lax.ppermute(right_a + far_a, "tp", turned(1))
    left_b = lax.ppermute(left_b + far_b, "tp", turned(-1))
    return total_call(own_a, left_a, right_a, own_b, left_b, right_b)


def solution(mesh):
    placed = (P("ctx", "tp"), P("ctx", "tp"), P("ctx", "tp"), P("tp"), P("tp", None))
    return jax.shard_map(
        on_device, mesh=mesh, in_specs=placed, out_specs=P(("ctx", "tp"), None), check_vma=False
    )
```

```python
import functools
import math

import jax
import jax.numpy as jnp
from jax import lax
from jax.experimental import pallas as pl
from jax.experimental.pallas import tpu as pltpu
from jax.sharding import PartitionSpec as P

H = 32
KVH = 8
HD = 128
GROUP = H // KVH
ROWS = 512
SPAN = 4
BLOCK = 64
N_CTX = 64
N_TP = 8
CHUNK = 256
LOG2E = 1.4426950408889634
SCALE = LOG2E / math.sqrt(HD)
MASKED = -1e30
F32 = jnp.float32
BF16 = jnp.bfloat16
VM = pl.BlockSpec(memory_space=pltpu.VMEM)
SM = pl.BlockSpec(memory_space=pltpu.SMEM)
NT = (((1,), (1,)), ((), ()))
TN = (((0,), (0,)), ((), ()))


def feature_map(x):
    return jnp.where(x > 0.0, x + 1.0, jnp.exp(jnp.minimum(x, 0.0)))


def split_two(x):
    high = x.astype(BF16)
    return high, (x - high.astype(F32)).astype(BF16)


def call(kernel, out_shape, cost, **kw):
    flops, read, exps = cost
    return pl.pallas_call(
        kernel,
        out_shape=out_shape,
        compiler_params=pltpu.CompilerParams(vmem_limit_bytes=24 * 1024 * 1024),
        cost_estimate=pl.CostEstimate(flops=flops, bytes_accessed=read, transcendentals=exps),
        **kw,
    )


def delta_kernel(kv_ref, d_ref, d16_ref):
    v = kv_ref[:, HD:]
    feat = feature_map(kv_ref[:, :HD].astype(F32))
    high, low = split_two(feat)
    delta = lax.dot_general(v, high, TN, preferred_element_type=F32) + lax.dot_general(
        v, low, TN, preferred_element_type=F32
    )
    norm = jnp.broadcast_to(jnp.sum(feat, axis=0, keepdims=True), (16, HD))
    d_ref[:HD, :] = delta
    d_ref[HD:, :] = norm
    d16_ref[:HD, :] = delta.astype(BF16)
    d16_ref[HD:, :] = norm.astype(BF16)


def delta_call(kv):
    return call(
        delta_kernel,
        (jax.ShapeDtypeStruct((HD + 16, HD), F32), jax.ShapeDtypeStruct((HD + 16, HD), BF16)),
        (2 * 2 * ROWS * HD * HD, 400000, ROWS * HD),
        in_specs=[VM],
        out_specs=(VM, VM),
    )(kv)


def values_and_ones(v):
    return jnp.concatenate([v, jnp.ones_like(v)], axis=1)


def own_kernel(q_ref, kv_ref, acc_ref, top_ref):
    k = kv_ref[:, :HD]
    wide = values_and_ones(kv_ref[:, HD:])
    for r in range(ROWS // CHUNK):
        rows = slice(r * CHUNK, (r + 1) * CHUNK)
        seen = (r + 1) * CHUNK
        query_pos = r * CHUNK + lax.broadcasted_iota(jnp.int32, (CHUNK, seen), 0)
        key_pos = lax.broadcasted_iota(jnp.int32, (CHUNK, seen), 1)
        visible = key_pos <= query_pos
        for h in range(GROUP):
            q = q_ref[rows, h * HD : (h + 1) * HD]
            s = lax.dot_general(q, k[:seen], NT, preferred_element_type=F32)
            s = jnp.where(visible, s, MASKED)
            top = jnp.max(s, axis=1, keepdims=True)
            p = jnp.exp2((s - top) * SCALE).astype(BF16)
            acc_ref[h, rows, :] = jnp.dot(p, wide[:seen], preferred_element_type=F32)
            top_ref[h, rows, :] = jnp.broadcast_to(top, (CHUNK, HD))


def own_call(queries, kv):
    return call(
        own_kernel,
        (
            jax.ShapeDtypeStruct((GROUP, ROWS, 2 * HD), F32),
            jax.ShapeDtypeStruct((GROUP, ROWS, HD), F32),
        ),
        (GROUP * ROWS * ROWS * HD * 4, 4000000, GROUP * ROWS * ROWS),
        in_specs=[VM, VM],
        out_specs=(VM, VM),
    )(queries, kv)


def step_kernel(distance, place_ref, q_ref, kv_ref, acc_in, top_in, *rest):
    if distance == SPAN - 1:
        w_hbm, acc_ref, w_ref, sem = rest
        top_ref = None
        copy = pltpu.make_async_copy(w_hbm, w_ref, sem)
        copy.start()
    else:
        acc_ref, top_ref = rest

    @pl.when(place_ref[0] >= distance)
    def _():
        k = kv_ref[:, :HD]
        wide = values_and_ones(kv_ref[:, HD:])
        for r in range(ROWS // CHUNK):
            rows = slice(r * CHUNK, (r + 1) * CHUNK)
            for h in range(GROUP):
                q = q_ref[rows, h * HD : (h + 1) * HD]
                s = lax.dot_general(q, k, NT, preferred_element_type=F32)
                before = top_in[h, rows, :]
                top = jnp.maximum(before, jnp.max(s, axis=1, keepdims=True))
                shrink = jnp.exp2((before - top) * SCALE)
                p = jnp.exp2((s - jnp.concatenate([top] * SPAN, axis=1)) * SCALE).astype(BF16)
                pv = jnp.dot(p, wide, preferred_element_type=F32)
                acc_ref[h, rows, :] = acc_in[h, rows, :] * jnp.concatenate([shrink, shrink], axis=1) + pv
                if top_ref is not None:
                    top_ref[h, rows, :] = top

    @pl.when(place_ref[0] < distance)
    def _():
        acc_ref[...] = acc_in[...]
        if top_ref is not None:
            top_ref[...] = top_in[...]

    if distance == SPAN - 1:
        copy.wait()


def step_call(distance, place, queries, kv, acc, top, *weights):
    last = distance == SPAN - 1
    state = (
        jax.ShapeDtypeStruct((GROUP, ROWS, 2 * HD), F32),
        jax.ShapeDtypeStruct((GROUP, ROWS, HD), F32),
    )
    return call(
        functools.partial(step_kernel, distance),
        (state[0], jax.ShapeDtypeStruct(weights[0].shape, BF16)) if last else state,
        (GROUP * ROWS * ROWS * HD * 4, 4000000, GROUP * ROWS * ROWS),
        in_specs=[SM] + [VM] * 4 + [pl.BlockSpec(memory_space=pl.ANY)] * len(weights),
        out_specs=(VM, VM),
        scratch_shapes=[pltpu.SemaphoreType.DMA] * len(weights),
    )(place, queries, kv, acc, top, *weights)


def merge_kernel(place_ref, gate_ref, q_ref, acc_ref, mem0, mem1, keep_ref, send_ref, out_ref):
    x = place_ref[1]
    core = place_ref[2]
    mem = mem0[...] + mem1[...].astype(F32)
    mem = jnp.concatenate([mem[:HD, :], jnp.broadcast_to(mem[HD : HD + 1, :], (HD, HD))], axis=0)
    mem_high, mem_low = split_two(mem)
    mem_twice = jnp.concatenate([mem_high, mem_high], axis=1)
    for h in range(GROUP):
        gate = jax.nn.sigmoid(jnp.full((1, HD), gate_ref[h], F32))
        feat = feature_map(q_ref[:, h * HD : (h + 1) * HD].astype(F32))
        high, low = split_two(feat)
        both = jnp.concatenate([high, low], axis=1)
        read = lax.dot_general(both, mem_twice, NT, preferred_element_type=F32)
        read = read + lax.dot_general(high, mem_low, NT, preferred_element_type=F32)
        retrieved = read[:, :HD] / jnp.maximum(read[:, HD:], 1.0)
        local = acc_ref[h, :, :HD] / acc_ref[h, :, HD:]
        out_ref[:, h * HD : (h + 1) * HD] = (gate * retrieved + (1.0 - gate) * local).astype(BF16)
    for b in range(N_TP // 2):
        chip = (x + b) % (N_TP // 2)
        mine = pl.multiple_of((2 * chip + core) * BLOCK, BLOCK)
        other = pl.multiple_of((2 * chip + 1 - core) * BLOCK, BLOCK)
        keep_ref[b * BLOCK : (b + 1) * BLOCK, :] = out_ref[pl.ds(mine, BLOCK), :]
        send_ref[b * BLOCK : (b + 1) * BLOCK, :] = out_ref[pl.ds(other, BLOCK), :]


def merge_call(place, gates, queries, acc, mem0, mem1):
    half = jax.ShapeDtypeStruct((ROWS // 2, GROUP * HD), BF16)
    return call(
        merge_kernel,
        (half, half),
        (6 * ROWS * GROUP * HD * HD * 2, 4000000, ROWS * GROUP * HD),
        in_specs=[SM, SM] + [VM] * 4,
        out_specs=(VM, VM),
        scratch_shapes=[pltpu.VMEM((ROWS, GROUP * HD), BF16)],
    )(place, gates, queries, acc, mem0, mem1)


def project_kernel(first, keep_ref, got_ref, w_own_ref, w_other_ref, own_ref, right_ref, far_ref, left_ref):
    width = own_ref.shape[1]
    tile = 512
    for j in range(width // tile):
        cols = slice(j * tile, (j + 1) * tile)
        from_w = slice(first + j * tile, first + (j + 1) * tile)
        out = jnp.dot(keep_ref[...], w_own_ref[:, from_w], preferred_element_type=F32)
        out = out + jnp.dot(got_ref[...], w_other_ref[:, from_w], preferred_element_type=F32)
        out = out.astype(BF16)
        for b, ref in enumerate((own_ref, right_ref, far_ref, left_ref)):
            ref[:, cols] = out[b * BLOCK : (b + 1) * BLOCK]


def project_call(first, keep, got, w_own, w_other):
    rows, depth = keep.shape
    half = w_own.shape[1] // 2
    return call(
        functools.partial(project_kernel, first),
        (jax.ShapeDtypeStruct((BLOCK, half), BF16),) * 4,
        (4 * rows * depth * half, 6000000, 0),
        in_specs=[VM] * 4,
        out_specs=(VM,) * 4,
    )(keep, got, w_own, w_other)


def total_kernel(own_a, left_a, right_a, own_b, left_b, right_b, out_ref):
    half = own_a.shape[1]
    for first, parts in ((0, (own_a, left_a, right_a)), (half, (own_b, left_b, right_b))):
        total = parts[0][...].astype(F32) + parts[1][...].astype(F32) + parts[2][...].astype(F32)
        out_ref[:, first : first + half] = total.astype(BF16)


def total_call(*parts):
    rows, half = parts[0].shape
    return call(
        total_kernel,
        jax.ShapeDtypeStruct((rows, 2 * half), BF16),
        (6 * rows * half, 2000000, 0),
        in_specs=[VM] * 6,
        out_specs=VM,
    )(*parts)


def along_z(step):
    return [(i, i + step) for i in range(N_CTX) if i // SPAN == (i + step) // SPAN]


def along_y(step):
    return [(i, i + 8 * step) for i in range(N_CTX - 8 * step)]


def swap(bit, size):
    return [(i, i ^ bit) for i in range(size)]


def after(x, *others):
    return lax.optimization_barrier((x, others))[0]


def turned(step):
    return [(i, (i + 2 * step) % N_TP) for i in range(N_TP)]


def on_device(queries, keys, values, gates, out_weight):
    ctx = lax.axis_index("ctx")
    tp = lax.axis_index("tp")
    place = jnp.stack([ctx % SPAN, tp // 2, tp % 2]).astype(jnp.int32)
    send = lambda x, route: lax.ppermute(x.astype(BF16), "ctx", route)
    kv = jnp.pad(keys, ((0, 0), (0, HD))) + jnp.pad(values, ((0, 0), (HD, 0)))
    delta, delta16 = delta_call(kv)
    w_other = lax.ppermute(out_weight, "tp", swap(1, N_TP))
    segment = [send(delta16, swap(k, N_CTX)) for k in (1, 2, 3)]
    kv1, kv2, kv3 = [send(kv, along_z(d)) for d in (1, 2, 3)]
    segment = delta + sum(part.astype(F32) for part in segment)
    other = send(segment, swap(4, N_CTX))
    acc, top = own_call(queries, kv)
    other = after(other, acc).astype(F32)
    line = segment + other
    start = jnp.where(ctx % 8 >= SPAN, other, 0.0)
    before = send(line, along_y(1))
    acc, top = step_call(1, place, queries, kv1, acc, top)
    before = after(before, acc).astype(F32)
    more = send(line + before, along_y(2))
    acc, top = step_call(2, place, queries, kv2, acc, top)
    before = before + after(more, acc).astype(F32)
    far = send(line + before, along_y(4))
    acc, w_other = step_call(3, place, queries, kv3, acc, top, w_other)
    keep, give = merge_call(place, gates, queries, acc, start + before, far)
    got = lax.ppermute(give, "tp", swap(1, N_TP))
    own_a, right_a, far_a, left_a = project_call(0, keep, got, out_weight, w_other)
    far_a = lax.ppermute(far_a, "tp", turned(1))
    left_a = lax.ppermute(left_a, "tp", turned(-1))
    own_b, right_b, far_b, left_b = project_call(own_a.shape[1], keep, got, out_weight, w_other)
    far_b = lax.ppermute(far_b, "tp", turned(-1))
    right_b = lax.ppermute(right_b, "tp", turned(1))
    right_a = lax.ppermute(right_a + far_a, "tp", turned(1))
    left_b = lax.ppermute(left_b + far_b, "tp", turned(-1))
    return total_call(own_a, left_a, right_a, own_b, left_b, right_b)


def solution(mesh):
    placed = (P("ctx", "tp"), P("ctx", "tp"), P("ctx", "tp"), P("tp"), P("tp", None))
    return jax.shard_map(
        on_device, mesh=mesh, in_specs=placed, out_specs=P(("ctx", "tp"), None), check_vma=False
    )
```

```python
import functools
import math

import jax
import jax.numpy as jnp
from jax import lax
from jax.experimental import pallas as pl
from jax.experimental.pallas import tpu as pltpu
from jax.sharding import PartitionSpec as P

H = 32
KVH = 8
HD = 128
GROUP = H // KVH
ROWS = 512
SPAN = 4
BLOCK = 64
N_CTX = 64
N_TP = 8
CHUNK = 256
LOG2E = 1.4426950408889634
SCALE = LOG2E / math.sqrt(HD)
MASKED = -1e30
F32 = jnp.float32
BF16 = jnp.bfloat16
VM = pl.BlockSpec(memory_space=pltpu.VMEM)
SM = pl.BlockSpec(memory_space=pltpu.SMEM)
NT = (((1,), (1,)), ((), ()))
TN = (((0,), (0,)), ((), ()))


def feature_map(x):
    return jnp.where(x > 0.0, x + 1.0, jnp.exp(jnp.minimum(x, 0.0)))


def split_two(x):
    high = x.astype(BF16)
    return high, (x - high.astype(F32)).astype(BF16)


def call(kernel, out_shape, cost, **kw):
    flops, read, exps = cost
    return pl.pallas_call(
        kernel,
        out_shape=out_shape,
        compiler_params=pltpu.CompilerParams(vmem_limit_bytes=16 * 1024 * 1024),
        cost_estimate=pl.CostEstimate(flops=flops, bytes_accessed=read, transcendentals=exps),
        **kw,
    )


def delta_kernel(kv_ref, d_ref, d16_ref):
    v = kv_ref[:, HD:]
    feat = feature_map(kv_ref[:, :HD].astype(F32))
    high, low = split_two(feat)
    delta = lax.dot_general(v, high, TN, preferred_element_type=F32) + lax.dot_general(
        v, low, TN, preferred_element_type=F32
    )
    norm = jnp.broadcast_to(jnp.sum(feat, axis=0, keepdims=True), (16, HD))
    d_ref[:HD, :] = delta
    d_ref[HD:, :] = norm
    d16_ref[:HD, :] = delta.astype(BF16)
    d16_ref[HD:, :] = norm.astype(BF16)


def delta_call(kv):
    return call(
        delta_kernel,
        (jax.ShapeDtypeStruct((HD + 16, HD), F32), jax.ShapeDtypeStruct((HD + 16, HD), BF16)),
        (2 * 2 * ROWS * HD * HD, 400000, ROWS * HD),
        in_specs=[VM],
        out_specs=(VM, VM),
    )(kv)


def values_and_ones(v):
    return jnp.concatenate([v, jnp.ones_like(v)], axis=1)


def own_kernel(q_ref, kv_ref, acc_ref, top_ref):
    k = kv_ref[:, :HD]
    wide = values_and_ones(kv_ref[:, HD:])
    for r in range(ROWS // CHUNK):
        rows = slice(r * CHUNK, (r + 1) * CHUNK)
        seen = (r + 1) * CHUNK
        query_pos = r * CHUNK + lax.broadcasted_iota(jnp.int32, (CHUNK, seen), 0)
        key_pos = lax.broadcasted_iota(jnp.int32, (CHUNK, seen), 1)
        visible = key_pos <= query_pos
        for h in range(GROUP):
            q = q_ref[rows, h * HD : (h + 1) * HD]
            s = lax.dot_general(q, k[:seen], NT, preferred_element_type=F32)
            s = jnp.where(visible, s, MASKED)
            top = jnp.max(s, axis=1, keepdims=True)
            p = jnp.exp2((s - top) * SCALE).astype(BF16)
            acc_ref[h, rows, :] = jnp.dot(p, wide[:seen], preferred_element_type=F32)
            top_ref[h, rows, :] = jnp.broadcast_to(top, (CHUNK, HD))


def own_call(queries, kv):
    return call(
        own_kernel,
        (
            jax.ShapeDtypeStruct((GROUP, ROWS, 2 * HD), F32),
            jax.ShapeDtypeStruct((GROUP, ROWS, HD), F32),
        ),
        (GROUP * ROWS * ROWS * HD * 4, 4000000, GROUP * ROWS * ROWS),
        in_specs=[VM, VM],
        out_specs=(VM, VM),
    )(queries, kv)


def step_kernel(distance, place_ref, q_ref, kv_ref, acc_in, top_in, acc_ref, top_ref=None):
    @pl.when(place_ref[0] >= distance)
    def _():
        k = kv_ref[:, :HD]
        wide = values_and_ones(kv_ref[:, HD:])
        for r in range(ROWS // CHUNK):
            rows = slice(r * CHUNK, (r + 1) * CHUNK)
            for h in range(GROUP):
                q = q_ref[rows, h * HD : (h + 1) * HD]
                s = lax.dot_general(q, k, NT, preferred_element_type=F32)
                before = top_in[h, rows, :]
                top = jnp.maximum(before, jnp.max(s, axis=1, keepdims=True))
                shrink = jnp.exp2((before - top) * SCALE)
                p = jnp.exp2((s - jnp.concatenate([top] * SPAN, axis=1)) * SCALE).astype(BF16)
                pv = jnp.dot(p, wide, preferred_element_type=F32)
                acc_ref[h, rows, :] = acc_in[h, rows, :] * jnp.concatenate([shrink, shrink], axis=1) + pv
                if top_ref is not None:
                    top_ref[h, rows, :] = top

    @pl.when(place_ref[0] < distance)
    def _():
        acc_ref[...] = acc_in[...]
        if top_ref is not None:
            top_ref[...] = top_in[...]


def step_call(distance, place, queries, kv, acc, top):
    state = (
        jax.ShapeDtypeStruct((GROUP, ROWS, 2 * HD), F32),
        jax.ShapeDtypeStruct((GROUP, ROWS, HD), F32),
    )
    kept = state[: 1 if distance == SPAN - 1 else 2]
    return call(
        functools.partial(step_kernel, distance),
        kept,
        (GROUP * ROWS * ROWS * HD * 4, 4000000, GROUP * ROWS * ROWS),
        in_specs=[SM] + [VM] * 4,
        out_specs=(VM,) * len(kept),
    )(place, queries, kv, acc, top)


def stage_kernel(w_hbm, w_ref, sem):
    copy = pltpu.make_async_copy(w_hbm, w_ref, sem)
    copy.start()
    copy.wait()


def stage_call(w):
    return call(
        stage_kernel,
        jax.ShapeDtypeStruct(w.shape, w.dtype),
        (0, 8000000, 0),
        in_specs=[pl.BlockSpec(memory_space=pl.ANY)],
        out_specs=VM,
        scratch_shapes=[pltpu.SemaphoreType.DMA],
    )(w)


def merge_kernel(place_ref, gate_ref, q_ref, acc_ref, mem0, mem1, keep_ref, send_ref, out_ref):
    x = place_ref[1]
    core = place_ref[2]
    mem = mem0[...] + mem1[...].astype(F32)
    mem = jnp.concatenate([mem[:HD, :], jnp.broadcast_to(mem[HD : HD + 1, :], (HD, HD))], axis=0)
    mem_high, mem_low = split_two(mem)
    mem_twice = jnp.concatenate([mem_high, mem_high], axis=1)
    for h in range(GROUP):
        gate = jax.nn.sigmoid(jnp.full((1, HD), gate_ref[h], F32))
        feat = feature_map(q_ref[:, h * HD : (h + 1) * HD].astype(F32))
        high, low = split_two(feat)
        both = jnp.concatenate([high, low], axis=1)
        read = lax.dot_general(both, mem_twice, NT, preferred_element_type=F32)
        read = read + lax.dot_general(high, mem_low, NT, preferred_element_type=F32)
        retrieved = read[:, :HD] / jnp.maximum(read[:, HD:], 1.0)
        local = acc_ref[h, :, :HD] / acc_ref[h, :, HD:]
        out_ref[:, h * HD : (h + 1) * HD] = (gate * retrieved + (1.0 - gate) * local).astype(BF16)
    for b in range(N_TP // 2):
        chip = (x + b) % (N_TP // 2)
        mine = pl.multiple_of((2 * chip + core) * BLOCK, BLOCK)
        other = pl.multiple_of((2 * chip + 1 - core) * BLOCK, BLOCK)
        keep_ref[b * BLOCK : (b + 1) * BLOCK, :] = out_ref[pl.ds(mine, BLOCK), :]
        send_ref[b * BLOCK : (b + 1) * BLOCK, :] = out_ref[pl.ds(other, BLOCK), :]


def merge_call(place, gates, queries, acc, mem0, mem1):
    half = jax.ShapeDtypeStruct((ROWS // 2, GROUP * HD), BF16)
    return call(
        merge_kernel,
        (half, half),
        (6 * ROWS * GROUP * HD * HD * 2, 4000000, ROWS * GROUP * HD),
        in_specs=[SM, SM] + [VM] * 4,
        out_specs=(VM, VM),
        scratch_shapes=[pltpu.VMEM((ROWS, GROUP * HD), BF16)],
    )(place, gates, queries, acc, mem0, mem1)


def project_kernel(first, keep_ref, got_ref, w_own_ref, w_other_ref, own_ref, right_ref, far_ref, left_ref):
    width = own_ref.shape[1]
    tile = 512
    for j in range(width // tile):
        cols = slice(j * tile, (j + 1) * tile)
        from_w = slice(first + j * tile, first + (j + 1) * tile)
        out = jnp.dot(keep_ref[...], w_own_ref[:, from_w], preferred_element_type=F32)
        out = out + jnp.dot(got_ref[...], w_other_ref[:, from_w], preferred_element_type=F32)
        out = out.astype(BF16)
        for b, ref in enumerate((own_ref, right_ref, far_ref, left_ref)):
            ref[:, cols] = out[b * BLOCK : (b + 1) * BLOCK]


def project_call(first, keep, got, w_own, w_other):
    rows, depth = keep.shape
    half = w_own.shape[1] // 2
    return call(
        functools.partial(project_kernel, first),
        (jax.ShapeDtypeStruct((BLOCK, half), BF16),) * 4,
        (4 * rows * depth * half, 6000000, 0),
        in_specs=[VM] * 4,
        out_specs=(VM,) * 4,
    )(keep, got, w_own, w_other)


def total_kernel(own_a, left_a, right_a, own_b, left_b, right_b, out_ref):
    half = own_a.shape[1]
    for first, parts in ((0, (own_a, left_a, right_a)), (half, (own_b, left_b, right_b))):
        total = parts[0][...].astype(F32) + parts[1][...].astype(F32) + parts[2][...].astype(F32)
        out_ref[:, first : first + half] = total.astype(BF16)


def total_call(*parts):
    rows, half = parts[0].shape
    return call(
        total_kernel,
        jax.ShapeDtypeStruct((rows, 2 * half), BF16),
        (6 * rows * half, 2000000, 0),
        in_specs=[VM] * 6,
        out_specs=VM,
    )(*parts)


def along_z(step):
    return [(i, i + step) for i in range(N_CTX) if i // SPAN == (i + step) // SPAN]


def along_y(step):
    return [(i, i + 8 * step) for i in range(N_CTX - 8 * step)]


def swap(bit, size):
    return [(i, i ^ bit) for i in range(size)]


def after(x, *others):
    return lax.optimization_barrier((x, others))[0]


def turned(step):
    return [(i, (i + 2 * step) % N_TP) for i in range(N_TP)]


def on_device(queries, keys, values, gates, out_weight):
    ctx = lax.axis_index("ctx")
    tp = lax.axis_index("tp")
    place = jnp.stack([ctx % SPAN, tp // 2, tp % 2]).astype(jnp.int32)
    send = lambda x, route: lax.ppermute(x.astype(BF16), "ctx", route)
    kv = jnp.pad(keys, ((0, 0), (0, HD))) + jnp.pad(values, ((0, 0), (HD, 0)))
    delta, delta16 = delta_call(kv)
    w_other = lax.ppermute(out_weight, "tp", swap(1, N_TP))
    kv1, kv2, kv3 = [send(kv, along_z(d)) for d in (1, 2, 3)]
    more = send(delta16, swap(1, N_CTX))
    acc, top = own_call(queries, kv)
    segment = delta + after(more, acc).astype(F32)
    more = send(segment, swap(2, N_CTX))
    acc, top = step_call(1, place, queries, kv1, acc, top)
    segment = segment + after(more, acc).astype(F32)
    other = send(segment, swap(4, N_CTX))
    acc, top = step_call(2, place, queries, kv2, acc, top)
    other = after(other, acc).astype(F32)
    line = segment + other
    start = jnp.where(ctx % 8 >= SPAN, other, 0.0)
    before = send(line, along_y(1))
    (acc,) = step_call(3, place, queries, kv3, acc, top)
    before = after(before, acc).astype(F32)
    before = before + send(line + before, along_y(2)).astype(F32)
    far = send(line + before, along_y(4))
    w_other = stage_call(w_other)
    far = after(far, w_other)
    keep, give = merge_call(place, gates, queries, acc, start + before, far)
    got = lax.ppermute(give, "tp", swap(1, N_TP))
    own_a, right_a, far_a, left_a = project_call(0, keep, got, out_weight, w_other)
    far_a = lax.ppermute(far_a, "tp", turned(1))
    left_a = lax.ppermute(left_a, "tp", turned(-1))
    own_b, right_b, far_b, left_b = project_call(own_a.shape[1], keep, got, out_weight, w_other)
    far_b = lax.ppermute(far_b, "tp", turned(-1))
    right_b = lax.ppermute(right_b, "tp", turned(1))
    right_a = lax.ppermute(right_a + far_a, "tp", turned(1))
    left_b = lax.ppermute(left_b + far_b, "tp", turned(-1))
    return total_call(own_a, left_a, right_a, own_b, left_b, right_b)


def solution(mesh):
    placed = (P("ctx", "tp"), P("ctx", "tp"), P("ctx", "tp"), P("tp"), P("tp", None))
    return jax.shard_map(
        on_device, mesh=mesh, in_specs=placed, out_specs=P(("ctx", "tp"), None), check_vma=False
    )
```

```python
import functools
import math

import jax
import jax.numpy as jnp
from jax import lax
from jax.experimental import pallas as pl
from jax.experimental.pallas import tpu as pltpu
from jax.sharding import PartitionSpec as P

H = 32
KVH = 8
HD = 128
GROUP = H // KVH
ROWS = 512
SPAN = 4
BLOCK = 64
N_CTX = 64
N_TP = 8
CHUNK = 256
LOG2E = 1.4426950408889634
SCALE = LOG2E / math.sqrt(HD)
MASKED = -1e30
F32 = jnp.float32
BF16 = jnp.bfloat16
VM = pl.BlockSpec(memory_space=pltpu.VMEM)
SM = pl.BlockSpec(memory_space=pltpu.SMEM)
NT = (((1,), (1,)), ((), ()))
TN = (((0,), (0,)), ((), ()))


def feature_map(x):
    return jnp.where(x > 0.0, x + 1.0, jnp.exp(jnp.minimum(x, 0.0)))


def split_two(x):
    high = x.astype(BF16)
    return high, (x - high.astype(F32)).astype(BF16)


def call(kernel, out_shape, cost, **kw):
    flops, read, exps = cost
    return pl.pallas_call(
        kernel,
        out_shape=out_shape,
        compiler_params=pltpu.CompilerParams(vmem_limit_bytes=16 * 1024 * 1024),
        cost_estimate=pl.CostEstimate(flops=flops, bytes_accessed=read, transcendentals=exps),
        **kw,
    )


def delta_kernel(kv_ref, d_ref, d16_ref):
    v = kv_ref[:, HD:]
    feat = feature_map(kv_ref[:, :HD].astype(F32))
    high, low = split_two(feat)
    delta = lax.dot_general(v, high, TN, preferred_element_type=F32) + lax.dot_general(
        v, low, TN, preferred_element_type=F32
    )
    norm = jnp.broadcast_to(jnp.sum(feat, axis=0, keepdims=True), (16, HD))
    d_ref[:HD, :] = delta
    d_ref[HD:, :] = norm
    d16_ref[:HD, :] = delta.astype(BF16)
    d16_ref[HD:, :] = norm.astype(BF16)


def delta_call(kv):
    return call(
        delta_kernel,
        (jax.ShapeDtypeStruct((HD + 16, HD), F32), jax.ShapeDtypeStruct((HD + 16, HD), BF16)),
        (2 * 2 * ROWS * HD * HD, 400000, ROWS * HD),
        in_specs=[VM],
        out_specs=(VM, VM),
    )(kv)


def values_and_ones(v):
    return jnp.concatenate([v, jnp.ones_like(v)], axis=1)


def own_kernel(q_ref, kv_ref, acc_ref, top_ref):
    k = kv_ref[:, :HD]
    wide = values_and_ones(kv_ref[:, HD:])
    for r in range(ROWS // CHUNK):
        rows = slice(r * CHUNK, (r + 1) * CHUNK)
        seen = (r + 1) * CHUNK
        query_pos = r * CHUNK + lax.broadcasted_iota(jnp.int32, (CHUNK, seen), 0)
        key_pos = lax.broadcasted_iota(jnp.int32, (CHUNK, seen), 1)
        visible = key_pos <= query_pos
        for h in range(GROUP):
            q = q_ref[rows, h * HD : (h + 1) * HD]
            s = lax.dot_general(q, k[:seen], NT, preferred_element_type=F32)
            s = jnp.where(visible, s, MASKED)
            top = jnp.max(s, axis=1, keepdims=True)
            p = jnp.exp2((s - top) * SCALE).astype(BF16)
            acc_ref[h, rows, :] = jnp.dot(p, wide[:seen], preferred_element_type=F32)
            top_ref[h, rows, :] = jnp.broadcast_to(top, (CHUNK, HD))


def own_call(queries, kv):
    return call(
        own_kernel,
        (
            jax.ShapeDtypeStruct((GROUP, ROWS, 2 * HD), F32),
            jax.ShapeDtypeStruct((GROUP, ROWS, HD), F32),
        ),
        (GROUP * ROWS * ROWS * HD * 4, 4000000, GROUP * ROWS * ROWS),
        in_specs=[VM, VM],
        out_specs=(VM, VM),
    )(queries, kv)


def step_kernel(distance, place_ref, q_ref, kv_ref, acc_in, top_in, acc_ref, top_ref=None):
    @pl.when(place_ref[0] >= distance)
    def _():
        k = kv_ref[:, :HD]
        wide = values_and_ones(kv_ref[:, HD:])
        for r in range(ROWS // CHUNK):
            rows = slice(r * CHUNK, (r + 1) * CHUNK)
            for h in range(GROUP):
                q = q_ref[rows, h * HD : (h + 1) * HD]
                s = lax.dot_general(q, k, NT, preferred_element_type=F32)
                before = top_in[h, rows, :]
                top = jnp.maximum(before, jnp.max(s, axis=1, keepdims=True))
                shrink = jnp.exp2((before - top) * SCALE)
                p = jnp.exp2((s - jnp.concatenate([top] * SPAN, axis=1)) * SCALE).astype(BF16)
                pv = jnp.dot(p, wide, preferred_element_type=F32)
                acc_ref[h, rows, :] = acc_in[h, rows, :] * jnp.concatenate([shrink, shrink], axis=1) + pv
                if top_ref is not None:
                    top_ref[h, rows, :] = top

    @pl.when(place_ref[0] < distance)
    def _():
        acc_ref[...] = acc_in[...]
        if top_ref is not None:
            top_ref[...] = top_in[...]


def step_call(distance, place, queries, kv, acc, top):
    state = (
        jax.ShapeDtypeStruct((GROUP, ROWS, 2 * HD), F32),
        jax.ShapeDtypeStruct((GROUP, ROWS, HD), F32),
    )
    kept = state[: 1 if distance == SPAN - 1 else 2]
    return call(
        functools.partial(step_kernel, distance),
        kept,
        (GROUP * ROWS * ROWS * HD * 4, 4000000, GROUP * ROWS * ROWS),
        in_specs=[SM] + [VM] * 4,
        out_specs=(VM,) * len(kept),
    )(place, queries, kv, acc, top)


def merge_kernel(
    place_ref, gate_ref, q_ref, acc_ref, mem0, mem1, mem2, mem3, w_hbm, keep_ref, send_ref, w_ref, out_ref, sem
):
    copy = pltpu.make_async_copy(w_hbm, w_ref, sem)
    copy.start()
    x = place_ref[1]
    core = place_ref[2]
    mem = mem0[...] + mem1[...].astype(F32) + (mem2[...].astype(F32) + mem3[...].astype(F32))
    mem = jnp.concatenate([mem[:HD, :], jnp.broadcast_to(mem[HD : HD + 1, :], (HD, HD))], axis=0)
    mem_high, mem_low = split_two(mem)
    mem_twice = jnp.concatenate([mem_high, mem_high], axis=1)
    for h in range(GROUP):
        gate = jax.nn.sigmoid(jnp.full((1, HD), gate_ref[h], F32))
        feat = feature_map(q_ref[:, h * HD : (h + 1) * HD].astype(F32))
        high, low = split_two(feat)
        both = jnp.concatenate([high, low], axis=1)
        read = lax.dot_general(both, mem_twice, NT, preferred_element_type=F32)
        read = read + lax.dot_general(high, mem_low, NT, preferred_element_type=F32)
        retrieved = read[:, :HD] / jnp.maximum(read[:, HD:], 1.0)
        local = acc_ref[h, :, :HD] / acc_ref[h, :, HD:]
        out_ref[:, h * HD : (h + 1) * HD] = (gate * retrieved + (1.0 - gate) * local).astype(BF16)
    for b in range(N_TP // 2):
        chip = (x + b) % (N_TP // 2)
        mine = pl.multiple_of((2 * chip + core) * BLOCK, BLOCK)
        other = pl.multiple_of((2 * chip + 1 - core) * BLOCK, BLOCK)
        keep_ref[b * BLOCK : (b + 1) * BLOCK, :] = out_ref[pl.ds(mine, BLOCK), :]
        send_ref[b * BLOCK : (b + 1) * BLOCK, :] = out_ref[pl.ds(other, BLOCK), :]
    copy.wait()


def merge_call(place, gates, queries, acc, mems, w):
    half = jax.ShapeDtypeStruct((ROWS // 2, GROUP * HD), BF16)
    return call(
        merge_kernel,
        (half, half, jax.ShapeDtypeStruct(w.shape, w.dtype)),
        (6 * ROWS * GROUP * HD * HD * 2, 8000000, ROWS * GROUP * HD),
        in_specs=[SM, SM] + [VM] * 6 + [pl.BlockSpec(memory_space=pl.ANY)],
        out_specs=(VM,) * 3,
        scratch_shapes=[pltpu.VMEM((ROWS, GROUP * HD), BF16), pltpu.SemaphoreType.DMA],
    )(place, gates, queries, acc, *mems, w)


def project_kernel(first, keep_ref, got_ref, w_own_ref, w_other_ref, own_ref, right_ref, far_ref, left_ref):
    width = own_ref.shape[1]
    tile = 512
    for j in range(width // tile):
        cols = slice(j * tile, (j + 1) * tile)
        from_w = slice(first + j * tile, first + (j + 1) * tile)
        out = jnp.dot(keep_ref[...], w_own_ref[:, from_w], preferred_element_type=F32)
        out = out + jnp.dot(got_ref[...], w_other_ref[:, from_w], preferred_element_type=F32)
        out = out.astype(BF16)
        for b, ref in enumerate((own_ref, right_ref, far_ref, left_ref)):
            ref[:, cols] = out[b * BLOCK : (b + 1) * BLOCK]


def project_call(first, keep, got, w_own, w_other):
    rows, depth = keep.shape
    half = w_own.shape[1] // 2
    return call(
        functools.partial(project_kernel, first),
        (jax.ShapeDtypeStruct((BLOCK, half), BF16),) * 4,
        (4 * rows * depth * half, 6000000, 0),
        in_specs=[VM] * 4,
        out_specs=(VM,) * 4,
    )(keep, got, w_own, w_other)


def total_kernel(own_a, left_a, right_a, own_b, left_b, right_b, out_ref):
    half = own_a.shape[1]
    for first, parts in ((0, (own_a, left_a, right_a)), (half, (own_b, left_b, right_b))):
        total = parts[0][...].astype(F32) + parts[1][...].astype(F32) + parts[2][...].astype(F32)
        out_ref[:, first : first + half] = total.astype(BF16)


def total_call(*parts):
    rows, half = parts[0].shape
    return call(
        total_kernel,
        jax.ShapeDtypeStruct((rows, 2 * half), BF16),
        (6 * rows * half, 2000000, 0),
        in_specs=[VM] * 6,
        out_specs=VM,
    )(*parts)


def along_z(step):
    return [(i, i + step) for i in range(N_CTX) if i // SPAN == (i + step) // SPAN]


def along_y(step):
    return [(i, i + 8 * step) for i in range(N_CTX - 8 * step)]


def swap(bit, size):
    return [(i, i ^ bit) for i in range(size)]


def after(x, *others):
    return lax.optimization_barrier((x, others))[0]


def turned(step):
    return [(i, (i + 2 * step) % N_TP) for i in range(N_TP)]


def on_device(queries, keys, values, gates, out_weight):
    ctx = lax.axis_index("ctx")
    tp = lax.axis_index("tp")
    place = jnp.stack([ctx % SPAN, tp // 2, tp % 2]).astype(jnp.int32)
    send = lambda x, route: lax.ppermute(x.astype(BF16), "ctx", route)
    kv = jnp.pad(keys, ((0, 0), (0, HD))) + jnp.pad(values, ((0, 0), (HD, 0)))
    delta, delta16 = delta_call(kv)
    w_other = lax.ppermute(out_weight, "tp", swap(1, N_TP))
    kv1, kv2, kv3 = [send(kv, along_z(d)) for d in (1, 2, 3)]
    got = send(delta16, along_y(1))
    acc, top = own_call(queries, kv)
    before = after(got, acc).astype(F32)
    got = send(delta + before, along_y(2))
    acc, top = step_call(1, place, queries, kv1, acc, top)
    before = before + after(got, acc).astype(F32)
    got = send(delta + before, along_y(4))
    acc, top = step_call(2, place, queries, kv2, acc, top)
    before = before + after(got, acc).astype(F32)
    lower = ctx % 8 < SPAN
    got = send(before + jnp.where(lower, delta, 0.0), swap(4, N_CTX))
    (acc,) = step_call(3, place, queries, kv3, acc, top)
    mem = before + after(got, acc).astype(F32)
    mems = [mem] + [send(mem, swap(k, N_CTX)) for k in (1, 2, 3)]
    keep, give, w_other = merge_call(place, gates, queries, acc, mems, w_other)
    got = lax.ppermute(give, "tp", swap(1, N_TP))
    own_a, right_a, far_a, left_a = project_call(0, keep, got, out_weight, w_other)
    far_a = lax.ppermute(far_a, "tp", turned(1))
    left_a = lax.ppermute(left_a, "tp", turned(-1))
    own_b, right_b, far_b, left_b = project_call(own_a.shape[1], keep, got, out_weight, w_other)
    far_b = lax.ppermute(far_b, "tp", turned(-1))
    right_b = lax.ppermute(right_b, "tp", turned(1))
    right_a = lax.ppermute(right_a + far_a, "tp", turned(1))
    left_b = lax.ppermute(left_b + far_b, "tp", turned(-1))
    return total_call(own_a, left_a, right_a, own_b, left_b, right_b)


def solution(mesh):
    placed = (P("ctx", "tp"), P("ctx", "tp"), P("ctx", "tp"), P("tp"), P("tp", None))
    return jax.shard_map(
        on_device, mesh=mesh, in_specs=placed, out_specs=P(("ctx", "tp"), None), check_vma=False
    )
```

```python
import functools
import math

import jax
import jax.numpy as jnp
from jax import lax
from jax.experimental import pallas as pl
from jax.experimental.pallas import tpu as pltpu
from jax.sharding import PartitionSpec as P

H = 32
KVH = 8
HD = 128
GROUP = H // KVH
ROWS = 512
SPAN = 4
BLOCK = 64
N_CTX = 64
N_TP = 8
CHUNK = 256
LOG2E = 1.4426950408889634
SCALE = LOG2E / math.sqrt(HD)
MASKED = -1e30
F32 = jnp.float32
BF16 = jnp.bfloat16
VM = pl.BlockSpec(memory_space=pltpu.VMEM)
SM = pl.BlockSpec(memory_space=pltpu.SMEM)
NT = (((1,), (1,)), ((), ()))
TN = (((0,), (0,)), ((), ()))


def feature_map(x):
    return jnp.where(x > 0.0, x + 1.0, jnp.exp(jnp.minimum(x, 0.0)))


def split_two(x):
    high = x.astype(BF16)
    return high, (x - high.astype(F32)).astype(BF16)


def call(kernel, out_shape, cost, **kw):
    flops, read, exps = cost
    return pl.pallas_call(
        kernel,
        out_shape=out_shape,
        compiler_params=pltpu.CompilerParams(vmem_limit_bytes=16 * 1024 * 1024),
        cost_estimate=pl.CostEstimate(flops=flops, bytes_accessed=read, transcendentals=exps),
        **kw,
    )


def delta_kernel(kv_ref, d_ref, d16_ref):
    v = kv_ref[:, HD:]
    feat = feature_map(kv_ref[:, :HD].astype(F32))
    high, low = split_two(feat)
    delta = lax.dot_general(v, high, TN, preferred_element_type=F32) + lax.dot_general(
        v, low, TN, preferred_element_type=F32
    )
    norm = jnp.broadcast_to(jnp.sum(feat, axis=0, keepdims=True), (16, HD))
    d_ref[:HD, :] = delta
    d_ref[HD:, :] = norm
    d16_ref[:HD, :] = delta.astype(BF16)
    d16_ref[HD:, :] = norm.astype(BF16)


def delta_call(kv):
    return call(
        delta_kernel,
        (jax.ShapeDtypeStruct((HD + 16, HD), F32), jax.ShapeDtypeStruct((HD + 16, HD), BF16)),
        (2 * 2 * ROWS * HD * HD, 400000, ROWS * HD),
        in_specs=[VM],
        out_specs=(VM, VM),
    )(kv)


def values_and_ones(v):
    return jnp.concatenate([v, jnp.ones_like(v)], axis=1)


def own_kernel(q_ref, kv_ref, acc_ref, top_ref):
    k = kv_ref[:, :HD]
    wide = values_and_ones(kv_ref[:, HD:])
    for r in range(ROWS // CHUNK):
        rows = slice(r * CHUNK, (r + 1) * CHUNK)
        seen = (r + 1) * CHUNK
        query_pos = r * CHUNK + lax.broadcasted_iota(jnp.int32, (CHUNK, seen), 0)
        key_pos = lax.broadcasted_iota(jnp.int32, (CHUNK, seen), 1)
        visible = key_pos <= query_pos
        for h in range(GROUP):
            q = q_ref[rows, h * HD : (h + 1) * HD]
            s = lax.dot_general(q, k[:seen], NT, preferred_element_type=F32)
            s = jnp.where(visible, s, MASKED)
            top = jnp.max(s, axis=1, keepdims=True)
            p = jnp.exp2((s - top) * SCALE).astype(BF16)
            acc_ref[h, rows, :] = jnp.dot(p, wide[:seen], preferred_element_type=F32)
            top_ref[h, rows, :] = jnp.broadcast_to(top, (CHUNK, HD))


def own_call(queries, kv):
    return call(
        own_kernel,
        (
            jax.ShapeDtypeStruct((GROUP, ROWS, 2 * HD), F32),
            jax.ShapeDtypeStruct((GROUP, ROWS, HD), F32),
        ),
        (GROUP * ROWS * ROWS * HD * 4, 4000000, GROUP * ROWS * ROWS),
        in_specs=[VM, VM],
        out_specs=(VM, VM),
    )(queries, kv)


def step_kernel(distance, place_ref, q_ref, kv_ref, acc_in, top_in, acc_ref, top_ref=None):
    @pl.when(place_ref[0] >= distance)
    def _():
        k = kv_ref[:, :HD]
        wide = values_and_ones(kv_ref[:, HD:])
        for r in range(ROWS // CHUNK):
            rows = slice(r * CHUNK, (r + 1) * CHUNK)
            for h in range(GROUP):
                q = q_ref[rows, h * HD : (h + 1) * HD]
                s = lax.dot_general(q, k, NT, preferred_element_type=F32)
                before = top_in[h, rows, :]
                top = jnp.maximum(before, jnp.max(s, axis=1, keepdims=True))
                shrink = jnp.exp2((before - top) * SCALE)
                p = jnp.exp2((s - jnp.concatenate([top] * SPAN, axis=1)) * SCALE).astype(BF16)
                pv = jnp.dot(p, wide, preferred_element_type=F32)
                acc_ref[h, rows, :] = acc_in[h, rows, :] * jnp.concatenate([shrink, shrink], axis=1) + pv
                if top_ref is not None:
                    top_ref[h, rows, :] = top

    @pl.when(place_ref[0] < distance)
    def _():
        acc_ref[...] = acc_in[...]
        if top_ref is not None:
            top_ref[...] = top_in[...]


def step_call(distance, place, queries, kv, acc, top):
    state = (
        jax.ShapeDtypeStruct((GROUP, ROWS, 2 * HD), F32),
        jax.ShapeDtypeStruct((GROUP, ROWS, HD), F32),
    )
    kept = state[: 1 if distance == SPAN - 1 else 2]
    return call(
        functools.partial(step_kernel, distance),
        kept,
        (GROUP * ROWS * ROWS * HD * 4, 4000000, GROUP * ROWS * ROWS),
        in_specs=[SM] + [VM] * 4,
        out_specs=(VM,) * len(kept),
    )(place, queries, kv, acc, top)


def stage_kernel(w_hbm, w_ref, sem):
    copy = pltpu.make_async_copy(w_hbm, w_ref, sem)
    copy.start()
    copy.wait()


def stage_call(w):
    return call(
        stage_kernel,
        jax.ShapeDtypeStruct(w.shape, w.dtype),
        (0, 8000000, 0),
        in_specs=[pl.BlockSpec(memory_space=pl.ANY)],
        out_specs=VM,
        scratch_shapes=[pltpu.SemaphoreType.DMA],
    )(w)


def merge_kernel(place_ref, gate_ref, q_ref, acc_ref, mem0, mem1, keep_ref, send_ref, out_ref):
    x = place_ref[1]
    core = place_ref[2]
    mem = mem0[...] + mem1[...].astype(F32)
    mem = jnp.concatenate([mem[:HD, :], jnp.broadcast_to(mem[HD : HD + 1, :], (HD, HD))], axis=0)
    mem_high, mem_low = split_two(mem)
    mem_twice = jnp.concatenate([mem_high, mem_high], axis=1)
    for h in range(GROUP):
        gate = jax.nn.sigmoid(jnp.full((1, HD), gate_ref[h], F32))
        feat = feature_map(q_ref[:, h * HD : (h + 1) * HD].astype(F32))
        high, low = split_two(feat)
        both = jnp.concatenate([high, low], axis=1)
        read = lax.dot_general(both, mem_twice, NT, preferred_element_type=F32)
        read = read + lax.dot_general(high, mem_low, NT, preferred_element_type=F32)
        retrieved = read[:, :HD] / jnp.maximum(read[:, HD:], 1.0)
        local = acc_ref[h, :, :HD] / acc_ref[h, :, HD:]
        out_ref[:, h * HD : (h + 1) * HD] = (gate * retrieved + (1.0 - gate) * local).astype(BF16)
    for b in range(N_TP // 2):
        chip = (x + b) % (N_TP // 2)
        mine = pl.multiple_of((2 * chip + core) * BLOCK, BLOCK)
        other = pl.multiple_of((2 * chip + 1 - core) * BLOCK, BLOCK)
        keep_ref[b * BLOCK : (b + 1) * BLOCK, :] = out_ref[pl.ds(mine, BLOCK), :]
        send_ref[b * BLOCK : (b + 1) * BLOCK, :] = out_ref[pl.ds(other, BLOCK), :]


def merge_call(place, gates, queries, acc, mem0, mem1):
    half = jax.ShapeDtypeStruct((ROWS // 2, GROUP * HD), BF16)
    return call(
        merge_kernel,
        (half, half),
        (6 * ROWS * GROUP * HD * HD * 2, 4000000, ROWS * GROUP * HD),
        in_specs=[SM, SM] + [VM] * 4,
        out_specs=(VM, VM),
        scratch_shapes=[pltpu.VMEM((ROWS, GROUP * HD), BF16)],
    )(place, gates, queries, acc, mem0, mem1)


def project_kernel(first, keep_ref, got_ref, w_own_ref, w_other_ref, own_ref, right_ref, far_ref, left_ref):
    width = own_ref.shape[1]
    tile = 512
    for j in range(width // tile):
        cols = slice(j * tile, (j + 1) * tile)
        from_w = slice(first + j * tile, first + (j + 1) * tile)
        out = jnp.dot(keep_ref[...], w_own_ref[:, from_w], preferred_element_type=F32)
        out = out + jnp.dot(got_ref[...], w_other_ref[:, from_w], preferred_element_type=F32)
        out = out.astype(BF16)
        for b, ref in enumerate((own_ref, right_ref, far_ref, left_ref)):
            ref[:, cols] = out[b * BLOCK : (b + 1) * BLOCK]


def project_call(first, keep, got, w_own, w_other):
    rows, depth = keep.shape
    half = w_own.shape[1] // 2
    return call(
        functools.partial(project_kernel, first),
        (jax.ShapeDtypeStruct((BLOCK, half), BF16),) * 4,
        (4 * rows * depth * half, 6000000, 0),
        in_specs=[VM] * 4,
        out_specs=(VM,) * 4,
    )(keep, got, w_own, w_other)


def total_kernel(own_a, left_a, right_a, own_b, left_b, right_b, out_ref):
    half = own_a.shape[1]
    for first, parts in ((0, (own_a, left_a, right_a)), (half, (own_b, left_b, right_b))):
        total = parts[0][...].astype(F32) + parts[1][...].astype(F32) + parts[2][...].astype(F32)
        out_ref[:, first : first + half] = total.astype(BF16)


def total_call(*parts):
    rows, half = parts[0].shape
    return call(
        total_kernel,
        jax.ShapeDtypeStruct((rows, 2 * half), BF16),
        (6 * rows * half, 2000000, 0),
        in_specs=[VM] * 6,
        out_specs=VM,
    )(*parts)


def along_z(step):
    return [(i, i + step) for i in range(N_CTX) if i // SPAN == (i + step) // SPAN]


def along_y(step):
    return [(i, i + 8 * step) for i in range(N_CTX - 8 * step)]


def swap(bit, size):
    return [(i, i ^ bit) for i in range(size)]


def after(x, *others):
    return lax.optimization_barrier((x, others))[0]


def turned(step):
    return [(i, (i + 2 * step) % N_TP) for i in range(N_TP)]


def on_device(queries, keys, values, gates, out_weight):
    ctx = lax.axis_index("ctx")
    tp = lax.axis_index("tp")
    place = jnp.stack([ctx % SPAN, tp // 2, tp % 2]).astype(jnp.int32)
    send = lambda x, route: lax.ppermute(x.astype(BF16), "ctx", route)
    kv = jnp.pad(keys, ((0, 0), (0, HD))) + jnp.pad(values, ((0, 0), (HD, 0)))
    delta, delta16 = delta_call(kv)
    w_other = lax.ppermute(out_weight, "tp", swap(1, N_TP))
    segment = [send(delta16, swap(k, N_CTX)) for k in (1, 2, 3)]
    kv1, kv2, kv3 = [send(kv, along_z(d)) for d in (1, 2, 3)]
    segment = delta + sum(part.astype(F32) for part in segment)
    other = send(segment, swap(4, N_CTX)).astype(F32)
    line = segment + other
    start = jnp.where(ctx % 8 >= SPAN, other, 0.0)
    before = send(line, along_y(1))
    acc, top = own_call(queries, kv)
    before = after(before, acc).astype(F32)
    more = send(line + before, along_y(2))
    acc, top = step_call(1, place, queries, kv1, acc, top)
    before = before + after(more, acc).astype(F32)
    far = send(line + before, along_y(4))
    w_other = stage_call(after(w_other, acc))
    acc, top = step_call(2, place, queries, after(kv2, w_other), acc, top)
    (acc,) = step_call(3, place, queries, kv3, acc, top)
    keep, give = merge_call(place, gates, queries, acc, start + before, far)
    got = lax.ppermute(give, "tp", swap(1, N_TP))
    own_a, right_a, far_a, left_a = project_call(0, keep, got, out_weight, w_other)
    far_a = lax.ppermute(far_a, "tp", turned(1))
    left_a = lax.ppermute(left_a, "tp", turned(-1))
    own_b, right_b, far_b, left_b = project_call(own_a.shape[1], keep, got, out_weight, w_other)
    far_b = lax.ppermute(far_b, "tp", turned(-1))
    right_b = lax.ppermute(right_b, "tp", turned(1))
    right_a = lax.ppermute(right_a + far_a, "tp", turned(1))
    left_b = lax.ppermute(left_b + far_b, "tp", turned(-1))
    return total_call(own_a, left_a, right_a, own_b, left_b, right_b)


def solution(mesh):
    placed = (P("ctx", "tp"), P("ctx", "tp"), P("ctx", "tp"), P("tp"), P("tp", None))
    return jax.shard_map(
        on_device, mesh=mesh, in_specs=placed, out_specs=P(("ctx", "tp"), None), check_vma=False
    )
```

```python
import functools
import math

import jax
import jax.numpy as jnp
from jax import lax
from jax.experimental import pallas as pl
from jax.experimental.pallas import tpu as pltpu
from jax.sharding import PartitionSpec as P

H = 32
KVH = 8
HD = 128
GROUP = H // KVH
ROWS = 512
SPAN = 4
BLOCK = 64
N_CTX = 64
N_TP = 8
CHUNK = 256
LOG2E = 1.4426950408889634
SCALE = LOG2E / math.sqrt(HD)
MASKED = -1e30
F32 = jnp.float32
BF16 = jnp.bfloat16
VM = pl.BlockSpec(memory_space=pltpu.VMEM)
SM = pl.BlockSpec(memory_space=pltpu.SMEM)
NT = (((1,), (1,)), ((), ()))
TN = (((0,), (0,)), ((), ()))


def feature_map(x):
    return jnp.where(x > 0.0, x + 1.0, jnp.exp(jnp.minimum(x, 0.0)))


def split_two(x):
    high = x.astype(BF16)
    return high, (x - high.astype(F32)).astype(BF16)


def call(kernel, out_shape, cost, **kw):
    flops, read, exps = cost
    return pl.pallas_call(
        kernel,
        out_shape=out_shape,
        compiler_params=pltpu.CompilerParams(vmem_limit_bytes=16 * 1024 * 1024),
        cost_estimate=pl.CostEstimate(flops=flops, bytes_accessed=read, transcendentals=exps),
        **kw,
    )


def delta_kernel(kv_ref, d_ref, d16_ref):
    v = kv_ref[:, HD:]
    feat = feature_map(kv_ref[:, :HD].astype(F32))
    high, low = split_two(feat)
    delta = lax.dot_general(v, high, TN, preferred_element_type=F32) + lax.dot_general(
        v, low, TN, preferred_element_type=F32
    )
    norm = jnp.broadcast_to(jnp.sum(feat, axis=0, keepdims=True), (16, HD))
    d_ref[:HD, :] = delta
    d_ref[HD:, :] = norm
    d16_ref[:HD, :] = delta.astype(BF16)
    d16_ref[HD:, :] = norm.astype(BF16)


def delta_call(kv):
    return call(
        delta_kernel,
        (jax.ShapeDtypeStruct((HD + 16, HD), F32), jax.ShapeDtypeStruct((HD + 16, HD), BF16)),
        (2 * 2 * ROWS * HD * HD, 400000, ROWS * HD),
        in_specs=[VM],
        out_specs=(VM, VM),
    )(kv)


def values_and_ones(v):
    return jnp.concatenate([v, jnp.ones_like(v)], axis=1)


def own_kernel(q_ref, kv_ref, order, acc_ref, top_ref):
    del order
    k = kv_ref[:, :HD]
    wide = values_and_ones(kv_ref[:, HD:])
    for r in range(ROWS // CHUNK):
        rows = slice(r * CHUNK, (r + 1) * CHUNK)
        seen = (r + 1) * CHUNK
        query_pos = r * CHUNK + lax.broadcasted_iota(jnp.int32, (CHUNK, seen), 0)
        key_pos = lax.broadcasted_iota(jnp.int32, (CHUNK, seen), 1)
        visible = key_pos <= query_pos
        for h in range(GROUP):
            q = q_ref[rows, h * HD : (h + 1) * HD]
            s = lax.dot_general(q, k[:seen], NT, preferred_element_type=F32)
            s = jnp.where(visible, s, MASKED)
            top = jnp.max(s, axis=1, keepdims=True)
            p = jnp.exp2((s - top) * SCALE).astype(BF16)
            acc_ref[h, rows, :] = jnp.dot(p, wide[:seen], preferred_element_type=F32)
            top_ref[h, rows, :] = jnp.broadcast_to(top, (CHUNK, HD))


def own_call(queries, kv, order):
    return call(
        own_kernel,
        (
            jax.ShapeDtypeStruct((GROUP, ROWS, 2 * HD), F32),
            jax.ShapeDtypeStruct((GROUP, ROWS, HD), F32),
        ),
        (GROUP * ROWS * ROWS * HD * 4, 4000000, GROUP * ROWS * ROWS),
        in_specs=[VM, VM, pl.BlockSpec(memory_space=pl.ANY)],
        out_specs=(VM, VM),
    )(queries, kv, order)


def step_kernel(distance, place_ref, q_ref, kv_ref, acc_in, top_in, order, acc_ref, top_ref=None):
    del order

    @pl.when(place_ref[0] >= distance)
    def _():
        k = kv_ref[:, :HD]
        wide = values_and_ones(kv_ref[:, HD:])
        for r in range(ROWS // CHUNK):
            rows = slice(r * CHUNK, (r + 1) * CHUNK)
            for h in range(GROUP):
                q = q_ref[rows, h * HD : (h + 1) * HD]
                s = lax.dot_general(q, k, NT, preferred_element_type=F32)
                before = top_in[h, rows, :]
                top = jnp.maximum(before, jnp.max(s, axis=1, keepdims=True))
                shrink = jnp.exp2((before - top) * SCALE)
                p = jnp.exp2((s - jnp.concatenate([top] * SPAN, axis=1)) * SCALE).astype(BF16)
                pv = jnp.dot(p, wide, preferred_element_type=F32)
                acc_ref[h, rows, :] = acc_in[h, rows, :] * jnp.concatenate([shrink, shrink], axis=1) + pv
                if top_ref is not None:
                    top_ref[h, rows, :] = top

    @pl.when(place_ref[0] < distance)
    def _():
        acc_ref[...] = acc_in[...]
        if top_ref is not None:
            top_ref[...] = top_in[...]


def step_call(distance, place, queries, kv, acc, top, order):
    state = (
        jax.ShapeDtypeStruct((GROUP, ROWS, 2 * HD), F32),
        jax.ShapeDtypeStruct((GROUP, ROWS, HD), F32),
    )
    kept = state[: 1 if distance == SPAN - 1 else 2]
    return call(
        functools.partial(step_kernel, distance),
        kept,
        (GROUP * ROWS * ROWS * HD * 4, 4000000, GROUP * ROWS * ROWS),
        in_specs=[SM] + [VM] * 4 + [pl.BlockSpec(memory_space=pl.ANY)],
        out_specs=(VM,) * len(kept),
    )(place, queries, kv, acc, top, order)


def stage_kernel(w_hbm, w_ref, sem):
    copy = pltpu.make_async_copy(w_hbm, w_ref, sem)
    copy.start()
    copy.wait()


def stage_call(w):
    return call(
        stage_kernel,
        jax.ShapeDtypeStruct(w.shape, w.dtype),
        (0, 8000000, 0),
        in_specs=[pl.BlockSpec(memory_space=pl.ANY)],
        out_specs=VM,
        scratch_shapes=[pltpu.SemaphoreType.DMA],
    )(w)


def merge_kernel(place_ref, gate_ref, q_ref, acc_ref, mem0, mem1, mem2, mem3, keep_ref, send_ref, out_ref):
    x = place_ref[1]
    core = place_ref[2]
    mem = mem0[...] + mem1[...].astype(F32) + (mem2[...].astype(F32) + mem3[...].astype(F32))
    mem = jnp.concatenate([mem[:HD, :], jnp.broadcast_to(mem[HD : HD + 1, :], (HD, HD))], axis=0)
    mem_high, mem_low = split_two(mem)
    mem_twice = jnp.concatenate([mem_high, mem_high], axis=1)
    for h in range(GROUP):
        gate = jax.nn.sigmoid(jnp.full((1, HD), gate_ref[h], F32))
        feat = feature_map(q_ref[:, h * HD : (h + 1) * HD].astype(F32))
        high, low = split_two(feat)
        both = jnp.concatenate([high, low], axis=1)
        read = lax.dot_general(both, mem_twice, NT, preferred_element_type=F32)
        read = read + lax.dot_general(high, mem_low, NT, preferred_element_type=F32)
        retrieved = read[:, :HD] / jnp.maximum(read[:, HD:], 1.0)
        local = acc_ref[h, :, :HD] / acc_ref[h, :, HD:]
        out_ref[:, h * HD : (h + 1) * HD] = (gate * retrieved + (1.0 - gate) * local).astype(BF16)
    for b in range(N_TP // 2):
        chip = (x + b) % (N_TP // 2)
        mine = pl.multiple_of((2 * chip + core) * BLOCK, BLOCK)
        other = pl.multiple_of((2 * chip + 1 - core) * BLOCK, BLOCK)
        keep_ref[b * BLOCK : (b + 1) * BLOCK, :] = out_ref[pl.ds(mine, BLOCK), :]
        send_ref[b * BLOCK : (b + 1) * BLOCK, :] = out_ref[pl.ds(other, BLOCK), :]


def merge_call(place, gates, queries, acc, mems):
    half = jax.ShapeDtypeStruct((ROWS // 2, GROUP * HD), BF16)
    return call(
        merge_kernel,
        (half, half),
        (6 * ROWS * GROUP * HD * HD * 2, 4000000, ROWS * GROUP * HD),
        in_specs=[SM, SM] + [VM] * 6,
        out_specs=(VM, VM),
        scratch_shapes=[pltpu.VMEM((ROWS, GROUP * HD), BF16)],
    )(place, gates, queries, acc, *mems)


def project_kernel(first, keep_ref, got_ref, w_own_ref, w_other_ref, own_ref, right_ref, far_ref, left_ref):
    width = own_ref.shape[1]
    tile = 512
    for j in range(width // tile):
        cols = slice(j * tile, (j + 1) * tile)
        from_w = slice(first + j * tile, first + (j + 1) * tile)
        out = jnp.dot(keep_ref[...], w_own_ref[:, from_w], preferred_element_type=F32)
        out = out + jnp.dot(got_ref[...], w_other_ref[:, from_w], preferred_element_type=F32)
        out = out.astype(BF16)
        for b, ref in enumerate((own_ref, right_ref, far_ref, left_ref)):
            ref[:, cols] = out[b * BLOCK : (b + 1) * BLOCK]


def project_call(first, keep, got, w_own, w_other):
    rows, depth = keep.shape
    half = w_own.shape[1] // 2
    return call(
        functools.partial(project_kernel, first),
        (jax.ShapeDtypeStruct((BLOCK, half), BF16),) * 4,
        (4 * rows * depth * half, 6000000, 0),
        in_specs=[VM] * 4,
        out_specs=(VM,) * 4,
    )(keep, got, w_own, w_other)


def total_kernel(own_a, left_a, right_a, own_b, left_b, right_b, out_ref):
    half = own_a.shape[1]
    for first, parts in ((0, (own_a, left_a, right_a)), (half, (own_b, left_b, right_b))):
        total = parts[0][...].astype(F32) + parts[1][...].astype(F32) + parts[2][...].astype(F32)
        out_ref[:, first : first + half] = total.astype(BF16)


def total_call(*parts):
    rows, half = parts[0].shape
    return call(
        total_kernel,
        jax.ShapeDtypeStruct((rows, 2 * half), BF16),
        (6 * rows * half, 2000000, 0),
        in_specs=[VM] * 6,
        out_specs=VM,
    )(*parts)


def along_z(step):
    return [(i, i + step) for i in range(N_CTX) if i // SPAN == (i + step) // SPAN]


def along_y(step):
    return [(i, i + 8 * step) for i in range(N_CTX - 8 * step)]


def swap(bit, size):
    return [(i, i ^ bit) for i in range(size)]


def other_half():
    return [(i, i // 8 * 8 + (i % 8 + (1 if i % SPAN == SPAN - 1 else 5)) % 8) for i in range(N_CTX)]


def after(x, *others):
    return lax.optimization_barrier((x, others))[0]


def turned(step):
    return [(i, (i + 2 * step) % N_TP) for i in range(N_TP)]


def on_device(queries, keys, values, gates, out_weight):
    ctx = lax.axis_index("ctx")
    tp = lax.axis_index("tp")
    place = jnp.stack([ctx % SPAN, tp // 2, tp % 2]).astype(jnp.int32)
    send = lambda x, route: lax.ppermute(x.astype(BF16), "ctx", route)
    kv = jnp.pad(keys, ((0, 0), (0, HD))) + jnp.pad(values, ((0, 0), (HD, 0)))
    delta, delta16 = delta_call(kv)
    w_other = lax.ppermute(out_weight, "tp", swap(1, N_TP))
    segment = [send(delta16, swap(k, N_CTX)) for k in (1, 2, 3)]
    kv1, kv2, kv3 = [send(kv, along_z(d)) for d in (1, 2, 3)]
    segment = delta + sum(part.astype(F32) for part in segment)
    other = send(segment, other_half())
    w_other = stage_call(w_other)
    other = after(other, w_other).astype(F32)
    line = segment + other
    start = jnp.where(ctx % 8 >= SPAN, other, 0.0)
    sent = line.astype(BF16)
    got = send(sent, swap(8, N_CTX))
    acc, top = own_call(queries, kv, sent)
    got = after(got, acc).astype(F32)
    start = start + jnp.where(ctx // 8 % 2 == 1, got, 0.0)
    sent = (line + got).astype(BF16)
    pairs = [send(sent, along_y(2 * k)) for k in (1, 2, 3)]
    acc, top = step_call(1, place, queries, kv1, acc, top, sent)
    acc, top = step_call(2, place, queries, kv2, acc, top, sent)
    (acc,) = step_call(3, place, queries, kv3, acc, top, sent)
    pairs = [after(part, acc) for part in pairs]
    keep, give = merge_call(place, gates, queries, acc, [start] + pairs)
    got = lax.ppermute(give, "tp", swap(1, N_TP))
    own_a, right_a, far_a, left_a = project_call(0, keep, got, out_weight, w_other)
    far_a = lax.ppermute(far_a, "tp", turned(1))
    left_a = lax.ppermute(left_a, "tp", turned(-1))
    own_b, right_b, far_b, left_b = project_call(own_a.shape[1], keep, got, out_weight, w_other)
    far_b = lax.ppermute(far_b, "tp", turned(-1))
    right_b = lax.ppermute(right_b, "tp", turned(1))
    right_a = lax.ppermute(right_a + far_a, "tp", turned(1))
    left_b = lax.ppermute(left_b + far_b, "tp", turned(-1))
    return total_call(own_a, left_a, right_a, own_b, left_b, right_b)


def solution(mesh):
    placed = (P("ctx", "tp"), P("ctx", "tp"), P("ctx", "tp"), P("tp"), P("tp", None))
    return jax.shard_map(
        on_device, mesh=mesh, in_specs=placed, out_specs=P(("ctx", "tp"), None), check_vma=False
    )
```

```python
import functools
import math

import jax
import jax.numpy as jnp
from jax import lax
from jax.experimental import pallas as pl
from jax.experimental.pallas import tpu as pltpu
from jax.sharding import PartitionSpec as P

H = 32
KVH = 8
HD = 128
GROUP = H // KVH
ROWS = 512
SPAN = 4
BLOCK = 64
N_CTX = 64
N_TP = 8
CHUNK = 256
LOG2E = 1.4426950408889634
SCALE = LOG2E / math.sqrt(HD)
MASKED = -1e30
F32 = jnp.float32
BF16 = jnp.bfloat16
VM = pl.BlockSpec(memory_space=pltpu.VMEM)
SM = pl.BlockSpec(memory_space=pltpu.SMEM)
NT = (((1,), (1,)), ((), ()))
TN = (((0,), (0,)), ((), ()))


def feature_map(x):
    return jnp.where(x > 0.0, x + 1.0, jnp.exp(jnp.minimum(x, 0.0)))


def split_two(x):
    high = x.astype(BF16)
    return high, (x - high.astype(F32)).astype(BF16)


def call(kernel, out_shape, cost, **kw):
    flops, read, exps = cost
    return pl.pallas_call(
        kernel,
        out_shape=out_shape,
        compiler_params=pltpu.CompilerParams(vmem_limit_bytes=16 * 1024 * 1024),
        cost_estimate=pl.CostEstimate(flops=flops, bytes_accessed=read, transcendentals=exps),
        **kw,
    )


def delta_kernel(kv_ref, d_ref, d16_ref):
    v = kv_ref[:, HD:]
    feat = feature_map(kv_ref[:, :HD].astype(F32))
    high, low = split_two(feat)
    delta = lax.dot_general(v, high, TN, preferred_element_type=F32) + lax.dot_general(
        v, low, TN, preferred_element_type=F32
    )
    norm = jnp.broadcast_to(jnp.sum(feat, axis=0, keepdims=True), (16, HD))
    d_ref[:HD, :] = delta
    d_ref[HD:, :] = norm
    d16_ref[:HD, :] = delta.astype(BF16)
    d16_ref[HD:, :] = norm.astype(BF16)


def delta_call(kv):
    return call(
        delta_kernel,
        (jax.ShapeDtypeStruct((HD + 16, HD), F32), jax.ShapeDtypeStruct((HD + 16, HD), BF16)),
        (2 * 2 * ROWS * HD * HD, 400000, ROWS * HD),
        in_specs=[VM],
        out_specs=(VM, VM),
    )(kv)


def values_and_ones(v):
    return jnp.concatenate([v, jnp.ones_like(v)], axis=1)


def own_kernel(q_ref, kv_ref, order, acc_ref, top_ref):
    del order
    k = kv_ref[:, :HD]
    wide = values_and_ones(kv_ref[:, HD:])
    for r in range(ROWS // CHUNK):
        rows = slice(r * CHUNK, (r + 1) * CHUNK)
        seen = (r + 1) * CHUNK
        query_pos = r * CHUNK + lax.broadcasted_iota(jnp.int32, (CHUNK, seen), 0)
        key_pos = lax.broadcasted_iota(jnp.int32, (CHUNK, seen), 1)
        visible = key_pos <= query_pos
        for h in range(GROUP):
            q = q_ref[rows, h * HD : (h + 1) * HD]
            s = lax.dot_general(q, k[:seen], NT, preferred_element_type=F32)
            s = jnp.where(visible, s, MASKED)
            top = jnp.max(s, axis=1, keepdims=True)
            p = jnp.exp2((s - top) * SCALE).astype(BF16)
            acc_ref[h, rows, :] = jnp.dot(p, wide[:seen], preferred_element_type=F32)
            top_ref[h, rows, :] = jnp.broadcast_to(top, (CHUNK, HD))


def own_call(queries, kv, order):
    return call(
        own_kernel,
        (
            jax.ShapeDtypeStruct((GROUP, ROWS, 2 * HD), F32),
            jax.ShapeDtypeStruct((GROUP, ROWS, HD), F32),
        ),
        (GROUP * ROWS * ROWS * HD * 4, 4000000, GROUP * ROWS * ROWS),
        in_specs=[VM, VM, pl.BlockSpec(memory_space=pl.ANY)],
        out_specs=(VM, VM),
    )(queries, kv, order)


def step_kernel(distance, place_ref, q_ref, kv_ref, acc_in, top_in, order, acc_ref, top_ref=None):
    del order

    @pl.when(place_ref[0] >= distance)
    def _():
        k = kv_ref[:, :HD]
        wide = values_and_ones(kv_ref[:, HD:])
        for r in range(ROWS // CHUNK):
            rows = slice(r * CHUNK, (r + 1) * CHUNK)
            for h in range(GROUP):
                q = q_ref[rows, h * HD : (h + 1) * HD]
                s = lax.dot_general(q, k, NT, preferred_element_type=F32)
                before = top_in[h, rows, :]
                top = jnp.maximum(before, jnp.max(s, axis=1, keepdims=True))
                shrink = jnp.exp2((before - top) * SCALE)
                p = jnp.exp2((s - jnp.concatenate([top] * SPAN, axis=1)) * SCALE).astype(BF16)
                pv = jnp.dot(p, wide, preferred_element_type=F32)
                acc_ref[h, rows, :] = acc_in[h, rows, :] * jnp.concatenate([shrink, shrink], axis=1) + pv
                if top_ref is not None:
                    top_ref[h, rows, :] = top

    @pl.when(place_ref[0] < distance)
    def _():
        acc_ref[...] = acc_in[...]
        if top_ref is not None:
            top_ref[...] = top_in[...]


def step_call(distance, place, queries, kv, acc, top, order):
    state = (
        jax.ShapeDtypeStruct((GROUP, ROWS, 2 * HD), F32),
        jax.ShapeDtypeStruct((GROUP, ROWS, HD), F32),
    )
    kept = state[: 1 if distance == SPAN - 1 else 2]
    return call(
        functools.partial(step_kernel, distance),
        kept,
        (GROUP * ROWS * ROWS * HD * 4, 4000000, GROUP * ROWS * ROWS),
        in_specs=[SM] + [VM] * 4 + [pl.BlockSpec(memory_space=pl.ANY)],
        out_specs=(VM,) * len(kept),
    )(place, queries, kv, acc, top, order)


def stage_kernel(w_hbm, w_ref, sem):
    copy = pltpu.make_async_copy(w_hbm, w_ref, sem)
    copy.start()
    copy.wait()


def stage_call(w):
    return call(
        stage_kernel,
        jax.ShapeDtypeStruct(w.shape, w.dtype),
        (0, 8000000, 0),
        in_specs=[pl.BlockSpec(memory_space=pl.ANY)],
        out_specs=VM,
        scratch_shapes=[pltpu.SemaphoreType.DMA],
    )(w)


def merge_kernel(place_ref, gate_ref, q_ref, acc_ref, mem0, mem1, mem2, mem3, keep_ref, send_ref, out_ref):
    x = place_ref[1]
    core = place_ref[2]
    mem = mem0[...] + mem1[...].astype(F32) + (mem2[...].astype(F32) + mem3[...].astype(F32))
    mem = jnp.concatenate([mem[:HD, :], jnp.broadcast_to(mem[HD : HD + 1, :], (HD, HD))], axis=0)
    mem_high, mem_low = split_two(mem)
    mem_twice = jnp.concatenate([mem_high, mem_high], axis=1)
    for h in range(GROUP):
        gate = jax.nn.sigmoid(jnp.full((1, HD), gate_ref[h], F32))
        feat = feature_map(q_ref[:, h * HD : (h + 1) * HD].astype(F32))
        high, low = split_two(feat)
        both = jnp.concatenate([high, low], axis=1)
        read = lax.dot_general(both, mem_twice, NT, preferred_element_type=F32)
        read = read + lax.dot_general(high, mem_low, NT, preferred_element_type=F32)
        retrieved = read[:, :HD] / jnp.maximum(read[:, HD:], 1.0)
        local = acc_ref[h, :, :HD] / acc_ref[h, :, HD:]
        out_ref[:, h * HD : (h + 1) * HD] = (gate * retrieved + (1.0 - gate) * local).astype(BF16)
    for b in range(N_TP // 2):
        chip = (x + b) % (N_TP // 2)
        mine = pl.multiple_of((2 * chip + core) * BLOCK, BLOCK)
        other = pl.multiple_of((2 * chip + 1 - core) * BLOCK, BLOCK)
        keep_ref[b * BLOCK : (b + 1) * BLOCK, :] = out_ref[pl.ds(mine, BLOCK), :]
        send_ref[b * BLOCK : (b + 1) * BLOCK, :] = out_ref[pl.ds(other, BLOCK), :]


def merge_call(place, gates, queries, acc, mems):
    half = jax.ShapeDtypeStruct((ROWS // 2, GROUP * HD), BF16)
    return call(
        merge_kernel,
        (half, half),
        (6 * ROWS * GROUP * HD * HD * 2, 4000000, ROWS * GROUP * HD),
        in_specs=[SM, SM] + [VM] * 6,
        out_specs=(VM, VM),
        scratch_shapes=[pltpu.VMEM((ROWS, GROUP * HD), BF16)],
    )(place, gates, queries, acc, *mems)


def project_kernel(first, keep_ref, got_ref, w_own_ref, w_other_ref, own_ref, right_ref, far_ref, left_ref):
    width = own_ref.shape[1]
    tile = 512
    for j in range(width // tile):
        cols = slice(j * tile, (j + 1) * tile)
        from_w = slice(first + j * tile, first + (j + 1) * tile)
        out = jnp.dot(keep_ref[...], w_own_ref[:, from_w], preferred_element_type=F32)
        out = out + jnp.dot(got_ref[...], w_other_ref[:, from_w], preferred_element_type=F32)
        out = out.astype(BF16)
        for b, ref in enumerate((own_ref, right_ref, far_ref, left_ref)):
            ref[:, cols] = out[b * BLOCK : (b + 1) * BLOCK]


def project_call(first, keep, got, w_own, w_other):
    rows, depth = keep.shape
    half = w_own.shape[1] // 2
    return call(
        functools.partial(project_kernel, first),
        (jax.ShapeDtypeStruct((BLOCK, half), BF16),) * 4,
        (4 * rows * depth * half, 6000000, 0),
        in_specs=[VM] * 4,
        out_specs=(VM,) * 4,
    )(keep, got, w_own, w_other)


def total_kernel(own_a, left_a, right_a, own_b, left_b, right_b, out_ref):
    half = own_a.shape[1]
    for first, parts in ((0, (own_a, left_a, right_a)), (half, (own_b, left_b, right_b))):
        total = parts[0][...].astype(F32) + parts[1][...].astype(F32) + parts[2][...].astype(F32)
        out_ref[:, first : first + half] = total.astype(BF16)


def total_call(*parts):
    rows, half = parts[0].shape
    return call(
        total_kernel,
        jax.ShapeDtypeStruct((rows, 2 * half), BF16),
        (6 * rows * half, 2000000, 0),
        in_specs=[VM] * 6,
        out_specs=VM,
    )(*parts)


def along_z(step):
    return [(i, i + step) for i in range(N_CTX) if i // SPAN == (i + step) // SPAN]


def along_y(step):
    return [(i, i + 8 * step) for i in range(N_CTX - 8 * step)]


def swap(bit, size):
    return [(i, i ^ bit) for i in range(size)]


def other_half():
    return [(i, i // 8 * 8 + (i % 8 + (1 if i % SPAN == SPAN - 1 else 5)) % 8) for i in range(N_CTX)]


def after(x, *others):
    return lax.optimization_barrier((x, others))[0]


def turned(step):
    return [(i, (i + 2 * step) % N_TP) for i in range(N_TP)]


def on_device(queries, keys, values, gates, out_weight):
    ctx = lax.axis_index("ctx")
    tp = lax.axis_index("tp")
    place = jnp.stack([ctx % SPAN, tp // 2, tp % 2]).astype(jnp.int32)
    send = lambda x, route: lax.ppermute(x.astype(BF16), "ctx", route)
    kv = jnp.pad(keys, ((0, 0), (0, HD))) + jnp.pad(values, ((0, 0), (HD, 0)))
    delta, delta16 = delta_call(kv)
    w_other = lax.ppermute(out_weight, "tp", swap(1, N_TP))
    segment = [send(delta16, swap(k, N_CTX)) for k in (1, 2, 3)]
    kv1, kv2, kv3 = [send(kv, along_z(d)) for d in (1, 2, 3)]
    segment = delta + sum(part.astype(F32) for part in segment)
    other = send(segment, other_half())
    w_other = stage_call(w_other)
    other = after(other, w_other).astype(F32)
    line = segment + other
    start = jnp.where(ctx % 8 >= SPAN, other, 0.0)
    sent = line.astype(BF16)
    got = send(sent, swap(8, N_CTX))
    acc, top = own_call(queries, kv, sent)
    acc, top = step_call(1, place, queries, kv1, acc, top, sent)
    got = after(got, acc).astype(F32)
    start = start + jnp.where(ctx // 8 % 2 == 1, got, 0.0)
    sent = (line + got).astype(BF16)
    pairs = [send(sent, along_y(2 * k)) for k in (3, 2, 1)]
    acc, top = step_call(2, place, queries, kv2, acc, top, sent)
    (acc,) = step_call(3, place, queries, kv3, acc, top, sent)
    pairs = [after(part, acc) for part in pairs]
    keep, give = merge_call(place, gates, queries, acc, [start] + pairs)
    got = lax.ppermute(give, "tp", swap(1, N_TP))
    own_a, right_a, far_a, left_a = project_call(0, keep, got, out_weight, w_other)
    far_a = lax.ppermute(far_a, "tp", turned(1))
    left_a = lax.ppermute(left_a, "tp", turned(-1))
    own_b, right_b, far_b, left_b = project_call(own_a.shape[1], keep, got, out_weight, w_other)
    far_b = lax.ppermute(far_b, "tp", turned(-1))
    right_b = lax.ppermute(right_b, "tp", turned(1))
    right_a = lax.ppermute(right_a + far_a, "tp", turned(1))
    left_b = lax.ppermute(left_b + far_b, "tp", turned(-1))
    return total_call(own_a, left_a, right_a, own_b, left_b, right_b)


def solution(mesh):
    placed = (P("ctx", "tp"), P("ctx", "tp"), P("ctx", "tp"), P("tp"), P("tp", None))
    return jax.shard_map(
        on_device, mesh=mesh, in_specs=placed, out_specs=P(("ctx", "tp"), None), check_vma=False
    )
```

```python
import functools
import math

import jax
import jax.numpy as jnp
from jax import lax
from jax.experimental import pallas as pl
from jax.experimental.pallas import tpu as pltpu
from jax.sharding import PartitionSpec as P

H = 32
KVH = 8
HD = 128
GROUP = H // KVH
ROWS = 512
SPAN = 4
BLOCK = 64
N_CTX = 64
N_TP = 8
CHUNK = 256
LOG2E = 1.4426950408889634
SCALE = LOG2E / math.sqrt(HD)
MASKED = -1e30
F32 = jnp.float32
BF16 = jnp.bfloat16
VM = pl.BlockSpec(memory_space=pltpu.VMEM)
SM = pl.BlockSpec(memory_space=pltpu.SMEM)
NT = (((1,), (1,)), ((), ()))
TN = (((0,), (0,)), ((), ()))


def feature_map(x):
    return jnp.where(x > 0.0, x + 1.0, jnp.exp(jnp.minimum(x, 0.0)))


def split_two(x):
    high = x.astype(BF16)
    return high, (x - high.astype(F32)).astype(BF16)


def call(kernel, out_shape, cost, **kw):
    flops, read, exps = cost
    return pl.pallas_call(
        kernel,
        out_shape=out_shape,
        compiler_params=pltpu.CompilerParams(vmem_limit_bytes=16 * 1024 * 1024),
        cost_estimate=pl.CostEstimate(flops=flops, bytes_accessed=read, transcendentals=exps),
        **kw,
    )


def delta_kernel(kv_ref, d_ref, d16_ref):
    v = kv_ref[:, HD:]
    feat = feature_map(kv_ref[:, :HD].astype(F32))
    high, low = split_two(feat)
    delta = lax.dot_general(v, high, TN, preferred_element_type=F32) + lax.dot_general(
        v, low, TN, preferred_element_type=F32
    )
    norm = jnp.broadcast_to(jnp.sum(feat, axis=0, keepdims=True), (16, HD))
    d_ref[:HD, :] = delta
    d_ref[HD:, :] = norm
    d16_ref[:HD, :] = delta.astype(BF16)
    d16_ref[HD:, :] = norm.astype(BF16)


def delta_call(kv):
    return call(
        delta_kernel,
        (jax.ShapeDtypeStruct((HD + 16, HD), F32), jax.ShapeDtypeStruct((HD + 16, HD), BF16)),
        (2 * 2 * ROWS * HD * HD, 400000, ROWS * HD),
        in_specs=[VM],
        out_specs=(VM, VM),
    )(kv)


def values_and_ones(v):
    return jnp.concatenate([v, jnp.ones_like(v)], axis=1)


def own_kernel(q_ref, kv_ref, order, acc_ref, top_ref):
    del order
    k = kv_ref[:, :HD]
    wide = values_and_ones(kv_ref[:, HD:])
    for r in range(ROWS // CHUNK):
        rows = slice(r * CHUNK, (r + 1) * CHUNK)
        seen = (r + 1) * CHUNK
        query_pos = r * CHUNK + lax.broadcasted_iota(jnp.int32, (CHUNK, seen), 0)
        key_pos = lax.broadcasted_iota(jnp.int32, (CHUNK, seen), 1)
        visible = key_pos <= query_pos
        for h in range(GROUP):
            q = q_ref[rows, h * HD : (h + 1) * HD]
            s = lax.dot_general(q, k[:seen], NT, preferred_element_type=F32)
            s = jnp.where(visible, s, MASKED)
            top = jnp.max(s, axis=1, keepdims=True)
            p = jnp.exp2((s - top) * SCALE).astype(BF16)
            acc_ref[h, rows, :] = jnp.dot(p, wide[:seen], preferred_element_type=F32)
            top_ref[h, rows, :] = jnp.broadcast_to(top, (CHUNK, HD))


def own_call(queries, kv, order):
    return call(
        own_kernel,
        (
            jax.ShapeDtypeStruct((GROUP, ROWS, 2 * HD), F32),
            jax.ShapeDtypeStruct((GROUP, ROWS, HD), F32),
        ),
        (GROUP * ROWS * ROWS * HD * 4, 4000000, GROUP * ROWS * ROWS),
        in_specs=[VM, VM, pl.BlockSpec(memory_space=pl.ANY)],
        out_specs=(VM, VM),
    )(queries, kv, order)


def step_kernel(distance, place_ref, gate_ref, q_ref, kv_ref, acc_in, top_in, order, acc_ref, top_ref):
    del order
    last = distance == SPAN - 1

    @pl.when(place_ref[0] >= distance)
    def _():
        k = kv_ref[:, :HD]
        wide = values_and_ones(kv_ref[:, HD:])
        for r in range(ROWS // CHUNK):
            rows = slice(r * CHUNK, (r + 1) * CHUNK)
            for h in range(GROUP):
                q = q_ref[rows, h * HD : (h + 1) * HD]
                s = lax.dot_general(q, k, NT, preferred_element_type=F32)
                before = top_in[h, rows, :]
                top = jnp.maximum(before, jnp.max(s, axis=1, keepdims=True))
                shrink = jnp.exp2((before - top) * SCALE)
                p = jnp.exp2((s - jnp.concatenate([top] * SPAN, axis=1)) * SCALE).astype(BF16)
                pv = jnp.dot(p, wide, preferred_element_type=F32)
                acc = acc_in[h, rows, :] * jnp.concatenate([shrink, shrink], axis=1) + pv
                if last:
                    share = 1.0 - jax.nn.sigmoid(jnp.full((1, HD), gate_ref[h], F32))
                    acc_ref[rows, h * HD : (h + 1) * HD] = share * (acc[:, :HD] / acc[:, HD:])
                else:
                    acc_ref[h, rows, :] = acc
                    top_ref[h, rows, :] = top

    @pl.when(place_ref[0] < distance)
    def _():
        if last:
            for h in range(GROUP):
                share = 1.0 - jax.nn.sigmoid(jnp.full((1, HD), gate_ref[h], F32))
                acc_ref[:, h * HD : (h + 1) * HD] = share * (acc_in[h, :, :HD] / acc_in[h, :, HD:])
        else:
            acc_ref[...] = acc_in[...]
            top_ref[...] = top_in[...]

    if last:
        for h in range(GROUP):
            feat = feature_map(q_ref[:, h * HD : (h + 1) * HD].astype(F32))
            high, low = split_two(feat)
            top_ref[:, 2 * h * HD : (2 * h + 1) * HD] = high
            top_ref[:, (2 * h + 1) * HD : (2 * h + 2) * HD] = low


def step_call(distance, place, gates, queries, kv, acc, top, order):
    last = distance == SPAN - 1
    out = (
        jax.ShapeDtypeStruct((ROWS, GROUP * HD), F32) if last else jax.ShapeDtypeStruct(acc.shape, F32),
        jax.ShapeDtypeStruct((ROWS, 2 * GROUP * HD), BF16) if last else jax.ShapeDtypeStruct(top.shape, F32),
    )
    return call(
        functools.partial(step_kernel, distance),
        out,
        (GROUP * ROWS * ROWS * HD * 4, 4000000, GROUP * ROWS * ROWS),
        in_specs=[SM, SM] + [VM] * 4 + [pl.BlockSpec(memory_space=pl.ANY)],
        out_specs=(VM, VM),
    )(place, gates, queries, kv, acc, top, order)


def stage_kernel(w_hbm, w_ref, sem):
    copy = pltpu.make_async_copy(w_hbm, w_ref, sem)
    copy.start()
    copy.wait()


def stage_call(w):
    return call(
        stage_kernel,
        jax.ShapeDtypeStruct(w.shape, w.dtype),
        (0, 8000000, 0),
        in_specs=[pl.BlockSpec(memory_space=pl.ANY)],
        out_specs=VM,
        scratch_shapes=[pltpu.SemaphoreType.DMA],
    )(w)


def merge_kernel(
    place_ref, gate_ref, feat_ref, local_ref, mem0, mem1, mem2, mem3, keep_ref, send_ref, out_ref
):
    x = place_ref[1]
    core = place_ref[2]
    mem = mem0[...] + mem1[...].astype(F32) + (mem2[...].astype(F32) + mem3[...].astype(F32))
    mem = jnp.concatenate([mem[:HD, :], jnp.broadcast_to(mem[HD : HD + 1, :], (HD, HD))], axis=0)
    mem_high, mem_low = split_two(mem)
    mem_twice = jnp.concatenate([mem_high, mem_high], axis=1)
    for h in range(GROUP):
        gate = jax.nn.sigmoid(jnp.full((1, HD), gate_ref[h], F32))
        both = feat_ref[:, 2 * h * HD : (2 * h + 2) * HD]
        read = lax.dot_general(both, mem_twice, NT, preferred_element_type=F32)
        read = read + lax.dot_general(both[:, :HD], mem_low, NT, preferred_element_type=F32)
        retrieved = read[:, :HD] / jnp.maximum(read[:, HD:], 1.0)
        cols = slice(h * HD, (h + 1) * HD)
        out_ref[:, cols] = (gate * retrieved + local_ref[:, cols]).astype(BF16)
    for b in range(N_TP // 2):
        chip = (x + b) % (N_TP // 2)
        mine = pl.multiple_of((2 * chip + core) * BLOCK, BLOCK)
        other = pl.multiple_of((2 * chip + 1 - core) * BLOCK, BLOCK)
        keep_ref[b * BLOCK : (b + 1) * BLOCK, :] = out_ref[pl.ds(mine, BLOCK), :]
        send_ref[b * BLOCK : (b + 1) * BLOCK, :] = out_ref[pl.ds(other, BLOCK), :]


def merge_call(place, gates, feats, local, mems):
    half = jax.ShapeDtypeStruct((ROWS // 2, GROUP * HD), BF16)
    return call(
        merge_kernel,
        (half, half),
        (6 * ROWS * GROUP * HD * HD * 2, 4000000, ROWS * GROUP * HD),
        in_specs=[SM, SM] + [VM] * 6,
        out_specs=(VM, VM),
        scratch_shapes=[pltpu.VMEM((ROWS, GROUP * HD), BF16)],
    )(place, gates, feats, local, *mems)


def own_heads_kernel(keep_ref, w_ref, out_ref):
    tile = 512
    for j in range(w_ref.shape[1] // tile):
        cols = slice(j * tile, (j + 1) * tile)
        out_ref[:, cols] = jnp.dot(keep_ref[...], w_ref[:, cols], preferred_element_type=F32)


def own_heads_call(keep, w):
    rows, depth = keep.shape
    return call(
        own_heads_kernel,
        jax.ShapeDtypeStruct((rows, w.shape[1]), F32),
        (2 * rows * depth * w.shape[1], 8000000, 0),
        in_specs=[VM] * 2,
        out_specs=VM,
    )(keep, w)


def project_kernel(first, part_ref, got_ref, w_ref, own_ref, right_ref, far_ref, left_ref):
    tile = 512
    for j in range(own_ref.shape[1] // tile):
        cols = slice(j * tile, (j + 1) * tile)
        from_w = slice(first + j * tile, first + (j + 1) * tile)
        out = part_ref[:, from_w] + jnp.dot(got_ref[...], w_ref[:, from_w], preferred_element_type=F32)
        out = out.astype(BF16)
        for b, ref in enumerate((own_ref, right_ref, far_ref, left_ref)):
            ref[:, cols] = out[b * BLOCK : (b + 1) * BLOCK]


def project_call(first, part, got, w):
    rows, depth = got.shape
    half = w.shape[1] // 2
    return call(
        functools.partial(project_kernel, first),
        (jax.ShapeDtypeStruct((BLOCK, half), BF16),) * 4,
        (2 * rows * depth * half, 4000000, 0),
        in_specs=[VM] * 3,
        out_specs=(VM,) * 4,
    )(part, got, w)


def total_kernel(own_a, left_a, right_a, own_b, left_b, right_b, out_ref):
    half = own_a.shape[1]
    for first, parts in ((0, (own_a, left_a, right_a)), (half, (own_b, left_b, right_b))):
        total = parts[0][...].astype(F32) + parts[1][...].astype(F32) + parts[2][...].astype(F32)
        out_ref[:, first : first + half] = total.astype(BF16)


def total_call(*parts):
    rows, half = parts[0].shape
    return call(
        total_kernel,
        jax.ShapeDtypeStruct((rows, 2 * half), BF16),
        (6 * rows * half, 2000000, 0),
        in_specs=[VM] * 6,
        out_specs=VM,
    )(*parts)


def along_z(step):
    return [(i, i + step) for i in range(N_CTX) if i // SPAN == (i + step) // SPAN]


def along_y(step):
    return [(i, i + 8 * step) for i in range(N_CTX - 8 * step)]


def swap(bit, size):
    return [(i, i ^ bit) for i in range(size)]


def other_half():
    return [(i, i // 8 * 8 + (i % 8 + (1 if i % SPAN == SPAN - 1 else 5)) % 8) for i in range(N_CTX)]


def after(x, *others):
    return lax.optimization_barrier((x, others))[0]


def turned(step):
    return [(i, (i + 2 * step) % N_TP) for i in range(N_TP)]


def on_device(queries, keys, values, gates, out_weight):
    ctx = lax.axis_index("ctx")
    tp = lax.axis_index("tp")
    place = jnp.stack([ctx % SPAN, tp // 2, tp % 2]).astype(jnp.int32)
    send = lambda x, route: lax.ppermute(x.astype(BF16), "ctx", route)
    kv = jnp.pad(keys, ((0, 0), (0, HD))) + jnp.pad(values, ((0, 0), (HD, 0)))
    delta, delta16 = delta_call(kv)
    w_other = lax.ppermute(out_weight, "tp", swap(1, N_TP))
    segment = [send(delta16, swap(k, N_CTX)) for k in (1, 2, 3)]
    kv1, kv2, kv3 = [send(kv, along_z(d)) for d in (1, 2, 3)]
    segment = delta + sum(part.astype(F32) for part in segment)
    other = send(segment, other_half())
    w_other = stage_call(w_other)
    other = after(other, w_other).astype(F32)
    line = segment + other
    start = jnp.where(ctx % 8 >= SPAN, other, 0.0)
    sent = line.astype(BF16)
    got = send(sent, swap(8, N_CTX))
    acc, top = own_call(queries, kv, sent)
    acc, top = step_call(1, place, gates, queries, kv1, acc, top, sent)
    got = after(got, acc).astype(F32)
    start = start + jnp.where(ctx // 8 % 2 == 1, got, 0.0)
    sent = (line + got).astype(BF16)
    pairs = [send(sent, along_y(2 * k)) for k in (3, 2, 1)]
    acc, top = step_call(2, place, gates, queries, kv2, acc, top, sent)
    local, feats = step_call(3, place, gates, queries, kv3, acc, top, sent)
    pairs = [after(part, local) for part in pairs]
    keep, give = merge_call(place, gates, feats, local, [start] + pairs)
    got = lax.ppermute(give, "tp", swap(1, N_TP))
    part = own_heads_call(keep, out_weight)
    got = after(got, part)
    own_a, right_a, far_a, left_a = project_call(0, part, got, w_other)
    far_a = lax.ppermute(far_a, "tp", turned(1))
    left_a = lax.ppermute(left_a, "tp", turned(-1))
    own_b, right_b, far_b, left_b = project_call(own_a.shape[1], part, got, w_other)
    far_b = lax.ppermute(far_b, "tp", turned(-1))
    right_b = lax.ppermute(right_b, "tp", turned(1))
    right_a = lax.ppermute(right_a + far_a, "tp", turned(1))
    left_b = lax.ppermute(left_b + far_b, "tp", turned(-1))
    return total_call(own_a, left_a, right_a, own_b, left_b, right_b)


def solution(mesh):
    placed = (P("ctx", "tp"), P("ctx", "tp"), P("ctx", "tp"), P("tp"), P("tp", None))
    return jax.shard_map(
        on_device, mesh=mesh, in_specs=placed, out_specs=P(("ctx", "tp"), None), check_vma=False
    )
```

```python
import functools
import math

import jax
import jax.numpy as jnp
from jax import lax
from jax.experimental import pallas as pl
from jax.experimental.pallas import tpu as pltpu
from jax.sharding import PartitionSpec as P

H = 32
KVH = 8
HD = 128
GROUP = H // KVH
ROWS = 512
SPAN = 4
BLOCK = 64
N_CTX = 64
N_TP = 8
CHUNK = 256
LOG2E = 1.4426950408889634
SCALE = LOG2E / math.sqrt(HD)
MASKED = -1e30
F32 = jnp.float32
BF16 = jnp.bfloat16
VM = pl.BlockSpec(memory_space=pltpu.VMEM)
SM = pl.BlockSpec(memory_space=pltpu.SMEM)
NT = (((1,), (1,)), ((), ()))
TN = (((0,), (0,)), ((), ()))


def feature_map(x):
    return jnp.where(x > 0.0, x + 1.0, jnp.exp(jnp.minimum(x, 0.0)))


def split_two(x):
    high = x.astype(BF16)
    return high, (x - high.astype(F32)).astype(BF16)


def call(kernel, out_shape, cost, **kw):
    flops, read, exps = cost
    return pl.pallas_call(
        kernel,
        out_shape=out_shape,
        compiler_params=pltpu.CompilerParams(vmem_limit_bytes=16 * 1024 * 1024),
        cost_estimate=pl.CostEstimate(flops=flops, bytes_accessed=read, transcendentals=exps),
        **kw,
    )


def delta_kernel(kv_ref, d_ref, d16_ref):
    v = kv_ref[:, HD:]
    feat = feature_map(kv_ref[:, :HD].astype(F32))
    high, low = split_two(feat)
    delta = lax.dot_general(v, high, TN, preferred_element_type=F32) + lax.dot_general(
        v, low, TN, preferred_element_type=F32
    )
    norm = jnp.broadcast_to(jnp.sum(feat, axis=0, keepdims=True), (16, HD))
    d_ref[:HD, :] = delta
    d_ref[HD:, :] = norm
    d16_ref[:HD, :] = delta.astype(BF16)
    d16_ref[HD:, :] = norm.astype(BF16)


def delta_call(kv):
    return call(
        delta_kernel,
        (jax.ShapeDtypeStruct((HD + 16, HD), F32), jax.ShapeDtypeStruct((HD + 16, HD), BF16)),
        (2 * 2 * ROWS * HD * HD, 400000, ROWS * HD),
        in_specs=[VM],
        out_specs=(VM, VM),
    )(kv)


def values_and_ones(v):
    return jnp.concatenate([v, jnp.ones_like(v)], axis=1)


def own_kernel(q_ref, kv_ref, order, acc_ref, top_ref):
    del order
    k = kv_ref[:, :HD]
    wide = values_and_ones(kv_ref[:, HD:])
    for r in range(ROWS // CHUNK):
        rows = slice(r * CHUNK, (r + 1) * CHUNK)
        seen = (r + 1) * CHUNK
        query_pos = r * CHUNK + lax.broadcasted_iota(jnp.int32, (CHUNK, seen), 0)
        key_pos = lax.broadcasted_iota(jnp.int32, (CHUNK, seen), 1)
        visible = key_pos <= query_pos
        for h in range(GROUP):
            q = q_ref[rows, h * HD : (h + 1) * HD]
            s = lax.dot_general(q, k[:seen], NT, preferred_element_type=F32)
            s = jnp.where(visible, s, MASKED)
            top = jnp.max(s, axis=1, keepdims=True)
            p = jnp.exp2((s - top) * SCALE).astype(BF16)
            acc_ref[h, rows, :] = jnp.dot(p, wide[:seen], preferred_element_type=F32)
            top_ref[h, rows, :] = jnp.broadcast_to(top, (CHUNK, HD))


def own_call(queries, kv, order):
    return call(
        own_kernel,
        (
            jax.ShapeDtypeStruct((GROUP, ROWS, 2 * HD), F32),
            jax.ShapeDtypeStruct((GROUP, ROWS, HD), F32),
        ),
        (GROUP * ROWS * ROWS * HD * 4, 4000000, GROUP * ROWS * ROWS),
        in_specs=[VM, VM, pl.BlockSpec(memory_space=pl.ANY)],
        out_specs=(VM, VM),
    )(queries, kv, order)


def step_kernel(distance, place_ref, gate_ref, q_ref, kv_ref, acc_in, top_in, order, acc_ref, top_ref):
    del order
    last = distance == SPAN - 1

    @pl.when(place_ref[0] >= distance)
    def _():
        k = kv_ref[:, :HD]
        wide = values_and_ones(kv_ref[:, HD:])
        for r in range(ROWS // CHUNK):
            rows = slice(r * CHUNK, (r + 1) * CHUNK)
            for h in range(GROUP):
                q = q_ref[rows, h * HD : (h + 1) * HD]
                s = lax.dot_general(q, k, NT, preferred_element_type=F32)
                before = top_in[h, rows, :]
                top = jnp.maximum(before, jnp.max(s, axis=1, keepdims=True))
                shrink = jnp.exp2((before - top) * SCALE)
                p = jnp.exp2((s - jnp.concatenate([top] * SPAN, axis=1)) * SCALE).astype(BF16)
                pv = jnp.dot(p, wide, preferred_element_type=F32)
                acc = acc_in[h, rows, :] * jnp.concatenate([shrink, shrink], axis=1) + pv
                if last:
                    share = 1.0 - jax.nn.sigmoid(jnp.full((1, HD), gate_ref[h], F32))
                    acc_ref[rows, h * HD : (h + 1) * HD] = share * (acc[:, :HD] / acc[:, HD:])
                else:
                    acc_ref[h, rows, :] = acc
                    top_ref[h, rows, :] = top

    @pl.when(place_ref[0] < distance)
    def _():
        if last:
            for h in range(GROUP):
                share = 1.0 - jax.nn.sigmoid(jnp.full((1, HD), gate_ref[h], F32))
                acc_ref[:, h * HD : (h + 1) * HD] = share * (acc_in[h, :, :HD] / acc_in[h, :, HD:])
        else:
            acc_ref[...] = acc_in[...]
            top_ref[...] = top_in[...]

    if last:
        for h in range(GROUP):
            feat = feature_map(q_ref[:, h * HD : (h + 1) * HD].astype(F32))
            high, low = split_two(feat)
            top_ref[:, 2 * h * HD : (2 * h + 1) * HD] = high
            top_ref[:, (2 * h + 1) * HD : (2 * h + 2) * HD] = low


def step_call(distance, place, gates, queries, kv, acc, top, order):
    last = distance == SPAN - 1
    out = (
        jax.ShapeDtypeStruct((ROWS, GROUP * HD), F32) if last else jax.ShapeDtypeStruct(acc.shape, F32),
        jax.ShapeDtypeStruct((ROWS, 2 * GROUP * HD), BF16) if last else jax.ShapeDtypeStruct(top.shape, F32),
    )
    return call(
        functools.partial(step_kernel, distance),
        out,
        (GROUP * ROWS * ROWS * HD * 4, 4000000, GROUP * ROWS * ROWS),
        in_specs=[SM, SM] + [VM] * 4 + [pl.BlockSpec(memory_space=pl.ANY)],
        out_specs=(VM, VM),
    )(place, gates, queries, kv, acc, top, order)


def stage_kernel(w_hbm, w_ref, sem):
    copy = pltpu.make_async_copy(w_hbm, w_ref, sem)
    copy.start()
    copy.wait()


def stage_call(w):
    return call(
        stage_kernel,
        jax.ShapeDtypeStruct(w.shape, w.dtype),
        (0, 8000000, 0),
        in_specs=[pl.BlockSpec(memory_space=pl.ANY)],
        out_specs=VM,
        scratch_shapes=[pltpu.SemaphoreType.DMA],
    )(w)


def merge_kernel(
    place_ref, gate_ref, feat_ref, local_ref, mem0, mem1, mem2, mem3, keep_ref, send_ref, out_ref
):
    x = place_ref[1]
    core = place_ref[2]
    mem = mem0[...] + mem1[...].astype(F32) + (mem2[...].astype(F32) + mem3[...].astype(F32))
    mem = jnp.concatenate([mem[:HD, :], jnp.broadcast_to(mem[HD : HD + 1, :], (HD, HD))], axis=0)
    mem_high, mem_low = split_two(mem)
    mem_twice = jnp.concatenate([mem_high, mem_high], axis=1)
    for h in range(GROUP):
        gate = jax.nn.sigmoid(jnp.full((1, HD), gate_ref[h], F32))
        both = feat_ref[:, 2 * h * HD : (2 * h + 2) * HD]
        read = lax.dot_general(both, mem_twice, NT, preferred_element_type=F32)
        read = read + lax.dot_general(both[:, :HD], mem_low, NT, preferred_element_type=F32)
        retrieved = read[:, :HD] / jnp.maximum(read[:, HD:], 1.0)
        cols = slice(h * HD, (h + 1) * HD)
        out_ref[:, cols] = (gate * retrieved + local_ref[:, cols]).astype(BF16)
    for b in range(N_TP // 2):
        chip = (x + b) % (N_TP // 2)
        mine = pl.multiple_of((2 * chip + core) * BLOCK, BLOCK)
        other = pl.multiple_of((2 * chip + 1 - core) * BLOCK, BLOCK)
        keep_ref[b * BLOCK : (b + 1) * BLOCK, :] = out_ref[pl.ds(mine, BLOCK), :]
        send_ref[b * BLOCK : (b + 1) * BLOCK, :] = out_ref[pl.ds(other, BLOCK), :]


def merge_call(place, gates, feats, local, mems):
    half = jax.ShapeDtypeStruct((ROWS // 2, GROUP * HD), BF16)
    return call(
        merge_kernel,
        (half, half),
        (6 * ROWS * GROUP * HD * HD * 2, 4000000, ROWS * GROUP * HD),
        in_specs=[SM, SM] + [VM] * 6,
        out_specs=(VM, VM),
        scratch_shapes=[pltpu.VMEM((ROWS, GROUP * HD), BF16)],
    )(place, gates, feats, local, *mems)


def own_heads_kernel(keep_ref, w_ref, out_ref):
    tile = 512
    for j in range(w_ref.shape[1] // tile):
        cols = slice(j * tile, (j + 1) * tile)
        out_ref[:, cols] = jnp.dot(keep_ref[...], w_ref[:, cols], preferred_element_type=F32)


def own_heads_call(keep, w):
    rows, depth = keep.shape
    return call(
        own_heads_kernel,
        jax.ShapeDtypeStruct((rows, w.shape[1]), F32),
        (2 * rows * depth * w.shape[1], 8000000, 0),
        in_specs=[VM] * 2,
        out_specs=VM,
    )(keep, w)


def project_kernel(first, part_ref, got_ref, w_ref, own_ref, right_ref, far_ref, left_ref):
    tile = 512
    for j in range(own_ref.shape[1] // tile):
        cols = slice(j * tile, (j + 1) * tile)
        from_w = slice(first + j * tile, first + (j + 1) * tile)
        out = part_ref[:, from_w] + jnp.dot(got_ref[...], w_ref[:, from_w], preferred_element_type=F32)
        out = out.astype(BF16)
        for b, ref in enumerate((own_ref, right_ref, far_ref, left_ref)):
            ref[:, cols] = out[b * BLOCK : (b + 1) * BLOCK]


def project_call(first, part, got, w):
    rows, depth = got.shape
    half = w.shape[1] // 2
    return call(
        functools.partial(project_kernel, first),
        (jax.ShapeDtypeStruct((BLOCK, half), BF16),) * 4,
        (2 * rows * depth * half, 4000000, 0),
        in_specs=[VM] * 3,
        out_specs=(VM,) * 4,
    )(part, got, w)


def total_kernel(own_a, left_a, right_a, own_b, left_b, right_b, out_ref):
    half = own_a.shape[1]
    for first, parts in ((0, (own_a, left_a, right_a)), (half, (own_b, left_b, right_b))):
        total = parts[0][...].astype(F32) + parts[1][...].astype(F32) + parts[2][...].astype(F32)
        out_ref[:, first : first + half] = total.astype(BF16)


def total_call(*parts):
    rows, half = parts[0].shape
    return call(
        total_kernel,
        jax.ShapeDtypeStruct((rows, 2 * half), BF16),
        (6 * rows * half, 2000000, 0),
        in_specs=[VM] * 6,
        out_specs=VM,
    )(*parts)


def along_z(step):
    return [(i, i + step) for i in range(N_CTX) if i // SPAN == (i + step) // SPAN]


def along_y(step):
    return [(i, i + 8 * step) for i in range(N_CTX - 8 * step)]


def swap(bit, size):
    return [(i, i ^ bit) for i in range(size)]


def other_half():
    return [(i, i // 8 * 8 + (i % 8 + (1 if i % SPAN == SPAN - 1 else 5)) % 8) for i in range(N_CTX)]


def two_pairs_on():
    return [(i, (i // 8 + 4 ^ 1) * 8 + i % 8) for i in range(N_CTX // 2)]


def after(x, *others):
    return lax.optimization_barrier((x, others))[0]


def turned(step):
    return [(i, (i + 2 * step) % N_TP) for i in range(N_TP)]


def on_device(queries, keys, values, gates, out_weight):
    ctx = lax.axis_index("ctx")
    tp = lax.axis_index("tp")
    place = jnp.stack([ctx % SPAN, tp // 2, tp % 2]).astype(jnp.int32)
    send = lambda x, route: lax.ppermute(x.astype(BF16), "ctx", route)
    kv = jnp.pad(keys, ((0, 0), (0, HD))) + jnp.pad(values, ((0, 0), (HD, 0)))
    delta, delta16 = delta_call(kv)
    w_other = lax.ppermute(out_weight, "tp", swap(1, N_TP))
    segment = [send(delta16, swap(k, N_CTX)) for k in (1, 2, 3)]
    kv1, kv2, kv3 = [send(kv, along_z(d)) for d in (1, 2, 3)]
    segment = delta + sum(part.astype(F32) for part in segment)
    other = send(segment, other_half())
    w_other = stage_call(w_other)
    other = after(other, w_other).astype(F32)
    line = segment + other
    start = jnp.where(ctx % 8 >= SPAN, other, 0.0)
    sent = line.astype(BF16)
    got = send(sent, swap(8, N_CTX))
    acc, top = own_call(queries, kv, sent)
    acc, top = step_call(1, place, gates, queries, kv1, acc, top, sent)
    got = after(got, acc).astype(F32)
    start = start + jnp.where(ctx // 8 % 2 == 1, got, 0.0)
    sent = (line + got).astype(BF16)
    pairs = [send(sent, route) for route in (two_pairs_on(), along_y(6), along_y(2))]
    acc, top = step_call(2, place, gates, queries, kv2, acc, top, sent)
    local, feats = step_call(3, place, gates, queries, kv3, acc, top, sent)
    pairs = [after(part, local) for part in pairs]
    keep, give = merge_call(place, gates, feats, local, [start] + pairs)
    got = lax.ppermute(give, "tp", swap(1, N_TP))
    part = own_heads_call(keep, out_weight)
    got = after(got, part)
    own_a, right_a, far_a, left_a = project_call(0, part, got, w_other)
    far_a = lax.ppermute(far_a, "tp", turned(1))
    left_a = lax.ppermute(left_a, "tp", turned(-1))
    own_b, right_b, far_b, left_b = project_call(own_a.shape[1], part, got, w_other)
    far_b = lax.ppermute(far_b, "tp", turned(-1))
    right_b = lax.ppermute(right_b, "tp", turned(1))
    right_a = lax.ppermute(right_a + far_a, "tp", turned(1))
    left_b = lax.ppermute(left_b + far_b, "tp", turned(-1))
    return total_call(own_a, left_a, right_a, own_b, left_b, right_b)


def solution(mesh):
    placed = (P("ctx", "tp"), P("ctx", "tp"), P("ctx", "tp"), P("tp"), P("tp", None))
    return jax.shard_map(
        on_device, mesh=mesh, in_specs=placed, out_specs=P(("ctx", "tp"), None), check_vma=False
    )
```

```python
import functools
import math

import jax
import jax.numpy as jnp
from jax import lax
from jax.experimental import pallas as pl
from jax.experimental.pallas import tpu as pltpu
from jax.sharding import PartitionSpec as P

H = 32
KVH = 8
HD = 128
GROUP = H // KVH
ROWS = 512
SPAN = 4
BLOCK = 64
N_CTX = 64
N_TP = 8
CHUNK = 256
LOG2E = 1.4426950408889634
SCALE = LOG2E / math.sqrt(HD)
MASKED = -1e30
F32 = jnp.float32
BF16 = jnp.bfloat16
VM = pl.BlockSpec(memory_space=pltpu.VMEM)
SM = pl.BlockSpec(memory_space=pltpu.SMEM)
NT = (((1,), (1,)), ((), ()))
TN = (((0,), (0,)), ((), ()))


def feature_map(x):
    return jnp.where(x > 0.0, x + 1.0, jnp.exp(jnp.minimum(x, 0.0)))


def split_two(x):
    high = x.astype(BF16)
    return high, (x - high.astype(F32)).astype(BF16)


def call(kernel, out_shape, cost, **kw):
    flops, read, exps = cost
    return pl.pallas_call(
        kernel,
        out_shape=out_shape,
        compiler_params=pltpu.CompilerParams(vmem_limit_bytes=16 * 1024 * 1024),
        cost_estimate=pl.CostEstimate(flops=flops, bytes_accessed=read, transcendentals=exps),
        **kw,
    )


def delta_kernel(kv_ref, d_ref, d16_ref):
    v = kv_ref[:, HD:]
    feat = feature_map(kv_ref[:, :HD].astype(F32))
    high, low = split_two(feat)
    delta = lax.dot_general(v, high, TN, preferred_element_type=F32) + lax.dot_general(
        v, low, TN, preferred_element_type=F32
    )
    norm = jnp.broadcast_to(jnp.sum(feat, axis=0, keepdims=True), (16, HD))
    d_ref[:HD, :] = delta
    d_ref[HD:, :] = norm
    d16_ref[:HD, :] = delta.astype(BF16)
    d16_ref[HD:, :] = norm.astype(BF16)


def delta_call(kv):
    return call(
        delta_kernel,
        (jax.ShapeDtypeStruct((HD + 16, HD), F32), jax.ShapeDtypeStruct((HD + 16, HD), BF16)),
        (2 * 2 * ROWS * HD * HD, 400000, ROWS * HD),
        in_specs=[VM],
        out_specs=(VM, VM),
    )(kv)


def values_and_ones(v):
    return jnp.concatenate([v, jnp.ones_like(v)], axis=1)


def own_kernel(q_ref, kv_ref, order, acc_ref, top_ref):
    del order
    k = kv_ref[:, :HD]
    wide = values_and_ones(kv_ref[:, HD:])
    for r in range(ROWS // CHUNK):
        rows = slice(r * CHUNK, (r + 1) * CHUNK)
        seen = (r + 1) * CHUNK
        query_pos = r * CHUNK + lax.broadcasted_iota(jnp.int32, (CHUNK, seen), 0)
        key_pos = lax.broadcasted_iota(jnp.int32, (CHUNK, seen), 1)
        visible = key_pos <= query_pos
        for h in range(GROUP):
            q = q_ref[rows, h * HD : (h + 1) * HD]
            s = lax.dot_general(q, k[:seen], NT, preferred_element_type=F32)
            s = jnp.where(visible, s, MASKED)
            top = jnp.max(s, axis=1, keepdims=True)
            p = jnp.exp2((s - top) * SCALE).astype(BF16)
            acc_ref[h, rows, :] = jnp.dot(p, wide[:seen], preferred_element_type=F32)
            top_ref[h, rows, :] = jnp.broadcast_to(top, (CHUNK, HD))


def own_call(queries, kv, order):
    return call(
        own_kernel,
        (
            jax.ShapeDtypeStruct((GROUP, ROWS, 2 * HD), F32),
            jax.ShapeDtypeStruct((GROUP, ROWS, HD), F32),
        ),
        (GROUP * ROWS * ROWS * HD * 4, 4000000, GROUP * ROWS * ROWS),
        in_specs=[VM, VM, pl.BlockSpec(memory_space=pl.ANY)],
        out_specs=(VM, VM),
    )(queries, kv, order)


def step_kernel(distance, place_ref, gate_ref, q_ref, kv_ref, acc_in, top_in, order, acc_ref, top_ref):
    del order
    last = distance == SPAN - 1

    @pl.when(place_ref[0] >= distance)
    def _():
        k = kv_ref[:, :HD]
        wide = values_and_ones(kv_ref[:, HD:])
        for r in range(ROWS // CHUNK):
            rows = slice(r * CHUNK, (r + 1) * CHUNK)
            for h in range(GROUP):
                q = q_ref[rows, h * HD : (h + 1) * HD]
                s = lax.dot_general(q, k, NT, preferred_element_type=F32)
                before = top_in[h, rows, :]
                top = jnp.maximum(before, jnp.max(s, axis=1, keepdims=True))
                shrink = jnp.exp2((before - top) * SCALE)
                p = jnp.exp2((s - jnp.concatenate([top] * SPAN, axis=1)) * SCALE).astype(BF16)
                pv = jnp.dot(p, wide, preferred_element_type=F32)
                acc = acc_in[h, rows, :] * jnp.concatenate([shrink, shrink], axis=1) + pv
                if last:
                    share = 1.0 - jax.nn.sigmoid(jnp.full((1, HD), gate_ref[h], F32))
                    acc_ref[rows, h * HD : (h + 1) * HD] = share * (acc[:, :HD] / acc[:, HD:])
                else:
                    acc_ref[h, rows, :] = acc
                    top_ref[h, rows, :] = top

    @pl.when(place_ref[0] < distance)
    def _():
        if last:
            for h in range(GROUP):
                share = 1.0 - jax.nn.sigmoid(jnp.full((1, HD), gate_ref[h], F32))
                acc_ref[:, h * HD : (h + 1) * HD] = share * (acc_in[h, :, :HD] / acc_in[h, :, HD:])
        else:
            acc_ref[...] = acc_in[...]
            top_ref[...] = top_in[...]

    if last:
        for h in range(GROUP):
            feat = feature_map(q_ref[:, h * HD : (h + 1) * HD].astype(F32))
            high, low = split_two(feat)
            top_ref[:, 2 * h * HD : (2 * h + 1) * HD] = high
            top_ref[:, (2 * h + 1) * HD : (2 * h + 2) * HD] = low


def step_call(distance, place, gates, queries, kv, acc, top, order):
    last = distance == SPAN - 1
    out = (
        jax.ShapeDtypeStruct((ROWS, GROUP * HD), F32) if last else jax.ShapeDtypeStruct(acc.shape, F32),
        jax.ShapeDtypeStruct((ROWS, 2 * GROUP * HD), BF16) if last else jax.ShapeDtypeStruct(top.shape, F32),
    )
    return call(
        functools.partial(step_kernel, distance),
        out,
        (GROUP * ROWS * ROWS * HD * 4, 4000000, GROUP * ROWS * ROWS),
        in_specs=[SM, SM] + [VM] * 4 + [pl.BlockSpec(memory_space=pl.ANY)],
        out_specs=(VM, VM),
    )(place, gates, queries, kv, acc, top, order)


def stage_kernel(w_hbm, w_ref, sem):
    copy = pltpu.make_async_copy(w_hbm, w_ref, sem)
    copy.start()
    copy.wait()


def stage_call(w):
    return call(
        stage_kernel,
        jax.ShapeDtypeStruct(w.shape, w.dtype),
        (0, 8000000, 0),
        in_specs=[pl.BlockSpec(memory_space=pl.ANY)],
        out_specs=VM,
        scratch_shapes=[pltpu.SemaphoreType.DMA],
    )(w)


def merge_kernel(
    place_ref, gate_ref, feat_ref, local_ref, mem0, mem1, mem2, mem3, keep_ref, send_ref, out_ref
):
    x = place_ref[1]
    core = place_ref[2]
    mem = mem0[...] + mem1[...].astype(F32) + (mem2[...].astype(F32) + mem3[...].astype(F32))
    mem = jnp.concatenate([mem[:HD, :], jnp.broadcast_to(mem[HD : HD + 1, :], (HD, HD))], axis=0)
    mem_high, mem_low = split_two(mem)
    mem_twice = jnp.concatenate([mem_high, mem_high], axis=1)
    for h in range(GROUP):
        gate = jax.nn.sigmoid(jnp.full((1, HD), gate_ref[h], F32))
        both = feat_ref[:, 2 * h * HD : (2 * h + 2) * HD]
        read = lax.dot_general(both, mem_twice, NT, preferred_element_type=F32)
        read = read + lax.dot_general(both[:, :HD], mem_low, NT, preferred_element_type=F32)
        retrieved = read[:, :HD] / jnp.maximum(read[:, HD:], 1.0)
        cols = slice(h * HD, (h + 1) * HD)
        out_ref[:, cols] = (gate * retrieved + local_ref[:, cols]).astype(BF16)
    for b in range(N_TP // 2):
        chip = (x + b) % (N_TP // 2)
        mine = pl.multiple_of((2 * chip + core) * BLOCK, BLOCK)
        other = pl.multiple_of((2 * chip + 1 - core) * BLOCK, BLOCK)
        keep_ref[b * BLOCK : (b + 1) * BLOCK, :] = out_ref[pl.ds(mine, BLOCK), :]
        send_ref[b * BLOCK : (b + 1) * BLOCK, :] = out_ref[pl.ds(other, BLOCK), :]


def merge_call(place, gates, feats, local, mems):
    half = jax.ShapeDtypeStruct((ROWS // 2, GROUP * HD), BF16)
    return call(
        merge_kernel,
        (half, half),
        (6 * ROWS * GROUP * HD * HD * 2, 4000000, ROWS * GROUP * HD),
        in_specs=[SM, SM] + [VM] * 6,
        out_specs=(VM, VM),
        scratch_shapes=[pltpu.VMEM((ROWS, GROUP * HD), BF16)],
    )(place, gates, feats, local, *mems)


def own_heads_kernel(keep_ref, w_ref, out_ref):
    tile = 512
    for j in range(w_ref.shape[1] // tile):
        cols = slice(j * tile, (j + 1) * tile)
        out_ref[:, cols] = jnp.dot(keep_ref[...], w_ref[:, cols], preferred_element_type=F32)


def own_heads_call(keep, w):
    rows, depth = keep.shape
    return call(
        own_heads_kernel,
        jax.ShapeDtypeStruct((rows, w.shape[1]), F32),
        (2 * rows * depth * w.shape[1], 8000000, 0),
        in_specs=[VM] * 2,
        out_specs=VM,
    )(keep, w)


def project_kernel(first, part_ref, got_ref, w_ref, own_ref, right_ref, far_ref, left_ref):
    tile = 512
    for j in range(own_ref.shape[1] // tile):
        cols = slice(j * tile, (j + 1) * tile)
        from_w = slice(first + j * tile, first + (j + 1) * tile)
        out = part_ref[:, from_w] + jnp.dot(got_ref[...], w_ref[:, from_w], preferred_element_type=F32)
        out = out.astype(BF16)
        for b, ref in enumerate((own_ref, right_ref, far_ref, left_ref)):
            ref[:, cols] = out[b * BLOCK : (b + 1) * BLOCK]


def project_call(first, part, got, w):
    rows, depth = got.shape
    half = w.shape[1] // 2
    return call(
        functools.partial(project_kernel, first),
        (jax.ShapeDtypeStruct((BLOCK, half), BF16),) * 4,
        (2 * rows * depth * half, 4000000, 0),
        in_specs=[VM] * 3,
        out_specs=(VM,) * 4,
    )(part, got, w)


def total_kernel(own_a, left_a, right_a, own_b, left_b, right_b, out_hbm, out_ref, sems):
    half = own_a.shape[1]
    tile = half // 2
    copies = []
    for i, (parts, at) in enumerate(
        (parts, at) for parts in ((own_b, left_b, right_b), (own_a, left_a, right_a)) for at in (0, tile)
    ):
        cols = slice(at, at + tile)
        first = at + (half if i < 2 else 0)
        total = parts[0][:, cols].astype(F32) + parts[1][:, cols].astype(F32) + parts[2][:, cols].astype(F32)
        out_ref[:, first : first + tile] = total.astype(BF16)
        copy = pltpu.make_async_copy(
            out_ref.at[:, first : first + tile], out_hbm.at[:, first : first + tile], sems.at[i]
        )
        copy.start()
        copies.append(copy)
    for copy in copies:
        copy.wait()


def total_call(*parts):
    rows, half = parts[0].shape
    return call(
        total_kernel,
        jax.ShapeDtypeStruct((rows, 2 * half), BF16),
        (6 * rows * half, 2000000, 0),
        in_specs=[VM] * 6,
        out_specs=pl.BlockSpec(memory_space=pl.ANY),
        scratch_shapes=[pltpu.VMEM((rows, 2 * half), BF16), pltpu.SemaphoreType.DMA((4,))],
    )(*parts)


def along_z(step):
    return [(i, i + step) for i in range(N_CTX) if i // SPAN == (i + step) // SPAN]


def along_y(step):
    return [(i, i + 8 * step) for i in range(N_CTX - 8 * step)]


def swap(bit, size):
    return [(i, i ^ bit) for i in range(size)]


def other_half():
    return [(i, i // 8 * 8 + (i % 8 + (1 if i % SPAN == SPAN - 1 else 5)) % 8) for i in range(N_CTX)]


def two_pairs_on():
    return [(i, (i // 8 + 4 ^ 1) * 8 + i % 8) for i in range(N_CTX // 2)]


def after(x, *others):
    return lax.optimization_barrier((x, others))[0]


def turned(step):
    return [(i, (i + 2 * step) % N_TP) for i in range(N_TP)]


def on_device(queries, keys, values, gates, out_weight):
    ctx = lax.axis_index("ctx")
    tp = lax.axis_index("tp")
    place = jnp.stack([ctx % SPAN, tp // 2, tp % 2]).astype(jnp.int32)
    send = lambda x, route: lax.ppermute(x.astype(BF16), "ctx", route)
    kv = jnp.pad(keys, ((0, 0), (0, HD))) + jnp.pad(values, ((0, 0), (HD, 0)))
    delta, delta16 = delta_call(kv)
    w_other = lax.ppermute(out_weight, "tp", swap(1, N_TP))
    segment = [send(delta16, swap(k, N_CTX)) for k in (1, 2, 3)]
    kv1, kv2, kv3 = [send(kv, along_z(d)) for d in (1, 2, 3)]
    segment = delta + sum(part.astype(F32) for part in segment)
    other = send(segment, other_half())
    w_other = stage_call(w_other)
    other = after(other, w_other).astype(F32)
    line = segment + other
    start = jnp.where(ctx % 8 >= SPAN, other, 0.0)
    sent = line.astype(BF16)
    got = send(sent, swap(8, N_CTX))
    acc, top = own_call(queries, kv, sent)
    acc, top = step_call(1, place, gates, queries, kv1, acc, top, sent)
    got = after(got, acc).astype(F32)
    start = start + jnp.where(ctx // 8 % 2 == 1, got, 0.0)
    sent = (line + got).astype(BF16)
    pairs = [send(sent, route) for route in (two_pairs_on(), along_y(6), along_y(2))]
    acc, top = step_call(2, place, gates, queries, kv2, acc, top, sent)
    local, feats = step_call(3, place, gates, queries, kv3, acc, top, sent)
    pairs = [after(part, local) for part in pairs]
    keep, give = merge_call(place, gates, feats, local, [start] + pairs)
    got = lax.ppermute(give, "tp", swap(1, N_TP))
    part = own_heads_call(keep, out_weight)
    got = after(got, part)
    own_a, right_a, far_a, left_a = project_call(0, part, got, w_other)
    far_a = lax.ppermute(far_a, "tp", turned(1))
    left_a = lax.ppermute(left_a, "tp", turned(-1))
    own_b, right_b, far_b, left_b = project_call(own_a.shape[1], part, got, w_other)
    far_b = lax.ppermute(far_b, "tp", turned(-1))
    right_b = lax.ppermute(right_b, "tp", turned(1))
    right_a = lax.ppermute(right_a + far_a, "tp", turned(1))
    left_b = lax.ppermute(left_b + far_b, "tp", turned(-1))
    return total_call(own_a, left_a, right_a, own_b, left_b, right_b)


def solution(mesh):
    placed = (P("ctx", "tp"), P("ctx", "tp"), P("ctx", "tp"), P("tp"), P("tp", None))
    return jax.shard_map(
        on_device, mesh=mesh, in_specs=placed, out_specs=P(("ctx", "tp"), None), check_vma=False
    )
```
